32 devices in a mesh: parts: 2 (over y), tmpl: 4 (over x, core), chan: 4 (over z).
Axes of the slice: x: 2, y: 2, z: 4, core: 2. Of those that a mesh axis runs over, the one named last changes fastest.
Arguments:
- waveforms: bfloat16 [384, 1536], P(('parts', 'tmpl', 'chan')), parts along dimension 0
- templates: bfloat16 [32, 8, 600], P(('parts', 'tmpl'), 'chan'), parts along dimension 0
- selection: int32 [8, 4, 4, 6], P(('parts', 'tmpl'), 'chan'), parts along dimension 0, may hold values from -1 to 11, as said below
- channel_list: int32 [32, 8], P(('parts', 'tmpl'), 'chan'), parts along dimension 0, may hold values from 0 to 23, as said below
- moveouts: int32 [32, 8], P(('parts', 'tmpl'), 'chan'), parts along dimension 0, may hold values from 0 to 424
- weights: int32 [32, 8], P(('parts', 'tmpl'), 'chan'), parts along dimension 0, may hold values from 1 to 3
Outputs:
- detection: float32 [32, 512], P(('parts', 'tmpl'), 'chan'), parts along dimension 0
The draws below stay inside these ranges and needn't reach their ends.
There are 2 independent parts, one for each index of `parts`. The reference program is written for one: setup_inputs(seed, part) draws one part's arguments, and reference() takes and returns one part's arrays. A program takes and returns all parts, laid end to end along the dimension named above; each array names one. Nothing has to cross between parts.
Inputs may be any that keep to these rules, and one draw needn't show every extreme that they name: `selection`: in each group of 6 slots the live entries come first, are distinct local rows, and number 1 to 6; in every channel group one owner receives 6 live slots from every recording device. `channel_list`: every entry names a live slot sent to the template's owner in the entry's channel group.
All inputs are finite; a program needn't handle non-finite values.
Results may differ from the reference program's by a relative error of at most 0.0003.
Values may be sent and summed in bfloat16 or wider, within the bound.
No kernel may reach another device: no remote copies, remote signals or barrier semaphores. Data moves between devices by JAX's collectives and lax.ppermute only.
A program may use at most 64 MiB of HBM per device.

```python
import jax
import jax.numpy as jnp
from jax import lax

TLEN = 600
LAGS = 512
MOVEOUT = 425
CHAN_DEV = 12
CAPACITY = 6
TMPL_DEV = 4
CHAN_SLOTS = 2
OWNERS = 4
COLUMNS = 4
WIN = 1536
TEMPLATES = 16
SLOTS = 8
CHANNELS = 192


def route_counts(key):
    first, second = jax.random.split(key, 2)
    counts = jax.random.randint(first, (OWNERS, COLUMNS, OWNERS), 1, CAPACITY + 1)
    fullest = jax.random.randint(second, (COLUMNS,), 0, OWNERS)
    owner_ids = jnp.arange(OWNERS)
    return jnp.where(owner_ids[None, None, :] == fullest[None, :, None], CAPACITY, counts)


def draw_selection(key, part):
    counts = route_counts(key)
    key = jax.random.fold_in(key, 11)
    keys = jax.random.split(key, OWNERS * COLUMNS * OWNERS)
    orders = jax.vmap(lambda single: jax.random.permutation(single, CHAN_DEV))(keys)[:, :CAPACITY]
    orders = orders.reshape(OWNERS, COLUMNS, OWNERS, CAPACITY)
    slot = jnp.arange(CAPACITY)
    return jnp.where(slot < counts[..., None], orders, -1).astype(jnp.int32)


def draw_channel_list(key, part):
    counts = route_counts(key)
    key = jax.random.fold_in(key, 12)
    first, second = jax.random.split(key, 2)
    owner = jnp.arange(TEMPLATES) // TMPL_DEV
    column = jnp.arange(SLOTS) // CHAN_SLOTS
    source = jax.random.randint(first, (TEMPLATES, SLOTS), 0, OWNERS)
    live = counts[source, column[None, :], owner[:, None]]
    slot = jax.random.randint(second, (TEMPLATES, SLOTS), 0, live)
    return (source * CAPACITY + slot).astype(jnp.int32)


def draw_waveforms(key, part):
    key = jax.random.fold_in(key, 3)
    first, second, third = jax.random.split(key, 3)
    row_scale = jnp.exp(jax.random.uniform(second, (CHANNELS, 1), minval=0.0, maxval=2.3026))
    envelope = jnp.exp(jax.random.uniform(third, (CHANNELS, WIN), minval=-0.7, maxval=0.7))
    base = jax.random.normal(first, (CHANNELS, WIN))
    return (base * row_scale * envelope).astype(jnp.bfloat16)


def draw_templates(key, part):
    key = jax.random.fold_in(key, 5)
    first, second = jax.random.split(key, 2)
    scale = jnp.exp(jax.random.uniform(second, (TEMPLATES, SLOTS, 1), minval=0.0, maxval=2.3026))
    base = jax.random.normal(first, (TEMPLATES, SLOTS, TLEN))
    return (base * scale).astype(jnp.bfloat16)


def with_ends(array, rng, smallest, largest):
    longest = array.shape.index(max(array.shape))
    spots = []
    for shift in (0, 1):
        where = [jax.random.randint(jax.random.fold_in(rng, axis), (), 0, length) for axis, length in enumerate(array.shape)]
        where[longest] = (where[longest] + shift) % array.shape[longest]
        spots.append(tuple(where))
    return array.at[spots[0]].set(smallest).at[spots[1]].set(largest)


def setup_inputs(seed: int = 0, part: int = 0) -> dict:
    streams_of = jax.random.split(jax.random.key(seed), 7)
    own_keys = jax.random.split(jax.random.fold_in(streams_of[6], part), 7)
    waveforms = draw_waveforms(jax.random.fold_in(jax.random.fold_in(streams_of[6], part), 71), part)
    templates = draw_templates(jax.random.fold_in(jax.random.fold_in(streams_of[6], part), 71), part)
    selection = draw_selection(jax.random.fold_in(jax.random.fold_in(streams_of[6], part), 71), part)
    channel_list = draw_channel_list(jax.random.fold_in(jax.random.fold_in(streams_of[6], part), 71), part)
    moveouts = with_ends(jax.random.randint(own_keys[4], (TEMPLATES, SLOTS), 0, MOVEOUT), jax.random.fold_in(own_keys[4], 1), 0, MOVEOUT - 1).astype(jnp.int32)
    weights = with_ends(jax.random.randint(own_keys[5], (TEMPLATES, SLOTS), 1, 4), jax.random.fold_in(own_keys[5], 1), 1, 3).astype(jnp.int32)
    return dict(waveforms=waveforms, templates=templates, selection=selection, channel_list=channel_list, moveouts=moveouts, weights=weights)


EPS = 1e-06

def normalized_scores(segments, kernels):
    tlen = kernels.shape[-1]
    count = segments.shape[0]
    seg = segments.astype(jnp.float32)
    ker = kernels.astype(jnp.float32)
    products = lax.conv_general_dilated(seg[None], ker.reshape(count, 1, tlen), (1,), 'VALID', feature_group_count=count, precision=lax.Precision.HIGHEST)[0]
    squares = seg * seg
    running = jnp.concatenate([jnp.zeros((count, 1), jnp.float32), jnp.cumsum(squares, axis=1)], axis=1)
    lags = products.shape[1]
    energy = running[:, tlen:tlen + lags] - running[:, :lags]
    power = lax.optimization_barrier(jnp.mean(ker * ker, axis=1, keepdims=True))
    return products / (jnp.sqrt(jnp.float32(tlen)) * jnp.sqrt((power + EPS) * (energy / tlen + EPS)))

def reference(waveforms, templates, selection, channel_list, moveouts, weights):
    column = (jnp.arange(SLOTS) // CHAN_SLOTS).astype(jnp.int32)
    span = LAGS + TLEN - 1

    def one_owner(owner):
        start = (owner * TMPL_DEV).astype(jnp.int32)
        lists = lax.dynamic_slice_in_dim(channel_list, start, TMPL_DEV, 0)
        shifts = lax.dynamic_slice_in_dim(moveouts, start, TMPL_DEV, 0)
        weight = lax.dynamic_slice_in_dim(weights, start, TMPL_DEV, 0).astype(jnp.float32)
        kernels = lax.dynamic_slice_in_dim(templates, start, TMPL_DEV, 0)
        source = lists // CAPACITY
        slot = lists % CAPACITY
        local = selection[source, column[None, :], owner, slot]
        channel = ((source * COLUMNS + column[None, :]) * CHAN_DEV + local).astype(jnp.int32)
        rows = waveforms[channel.reshape(-1)]

        def window(row, offset):
            return lax.dynamic_slice_in_dim(row, offset.astype(jnp.int32), span, 0)
        segments = jax.vmap(window)(rows, shifts.reshape(-1))
        scores = normalized_scores(segments, kernels.reshape(-1, TLEN)).reshape(TMPL_DEV, SLOTS, LAGS)
        partial_value = lax.optimization_barrier(jnp.sum(weight[:, :, None] * scores, axis=1))
        total = lax.optimization_barrier(jnp.sum(weight * weight, axis=1))
        return partial_value / jnp.sqrt(total)[:, None]
    stacks = lax.map(one_owner, jnp.arange(OWNERS, dtype=jnp.int32))
    return stacks.reshape(TEMPLATES, LAGS)
```

```python
import functools

import jax
import jax.numpy as jnp
from jax import lax
from jax.experimental import pallas as pl
from jax.experimental.pallas import tpu as pltpu
from jax.sharding import PartitionSpec as P

LAGS = 512
EPS = 1e-06
LANES = 128
PAD = 16


def exchange(value, axis, distance):
    size = lax.axis_size(axis)
    return lax.ppermute(value, axis, [(i, i ^ distance) for i in range(size)])


def prepare(tlen, templates, weights, bands, box, scale, rows):
    count, slots, _ = templates.shape
    depth = box.shape[1]
    blocks = depth // LANES
    rows[...] = jnp.zeros_like(rows)
    for m in range(count):
        rows[m * slots : (m + 1) * slots, :tlen] = templates[m].astype(jnp.float32)
    row = lax.broadcasted_iota(jnp.int32, (LANES, LANES), 0)
    lane = lax.broadcasted_iota(jnp.int32, (LANES, LANES), 1)
    late = lane >= row
    zero = jnp.zeros((LANES, LANES), jnp.float32)
    values = rows[...]
    power = jnp.sum(values * values, axis=1, keepdims=True) / tlen
    factor = 1.0 / (jnp.sqrt(jnp.float32(tlen)) * jnp.sqrt(power + EPS))
    groups = LAGS // LANES
    for p in range(count * slots):
        before = zero
        for d in range(blocks):
            if d * LANES < tlen:
                part = jnp.broadcast_to(rows[p : p + 1, d * LANES : (d + 1) * LANES], (LANES, LANES))
                now = pltpu.roll(part, 0, axis=1, stride=1, stride_axis=0)
            else:
                now = zero
            bands[p * LANES : (p + 1) * LANES, d * LANES : (d + 1) * LANES] = jnp.where(late, now, before).astype(jnp.bfloat16)
            before = now
        weight = weights[p % slots, p // slots].astype(jnp.float32)
        scale[p * groups : (p + 1) * groups, :] = jnp.broadcast_to(factor[p : p + 1] * weight, (groups, LANES))
    tap = lax.broadcasted_iota(jnp.int32, (LANES, depth), 1) - lax.broadcasted_iota(jnp.int32, (LANES, depth), 0)
    box[...] = jnp.where((tap >= 0) & (tap < tlen), 1.0, 0.0).astype(jnp.bfloat16)


def correlate(owners, columns, tlen, capacity, spot, lists, moveouts, weights, *refs):
    selections, refs = refs[:owners], refs[owners:]
    records, refs = refs[:owners], refs[owners:]
    bands, box, scale = refs[:3]
    outs, (lanes, taps, squares, stacks, blocks) = refs[3 : 3 + columns], refs[3 + columns :]
    owner, column = spot[0], spot[1]
    slots, count = lists.shape
    depth = box.shape[1]
    pieces = records[0].shape[1] // LANES
    high = records[0].shape[0]
    groups = LAGS // LANES
    for k in range(owners):
        wide = records[k][...].astype(jnp.float32)
        for d in range(pieces):
            lanes[k, d * PAD : d * PAD + high, :] = wide[:, d * LANES : (d + 1) * LANES]
        lanes[k, pieces * PAD :, :] = jnp.zeros((lanes.shape[1] - pieces * PAD, LANES), jnp.float32)
    reach = groups + depth // LANES - 1
    lane = lax.broadcasted_iota(jnp.int32, (reach, LANES), 1)
    for p in range(count * slots):
        m, j = p // slots, p % slots
        entry = lists[j, m]
        k = (entry // capacity) ^ owner
        slot = entry % capacity
        local = jnp.int32(0)
        for other in range(owners):
            local = jnp.where(k == other, selections[other][0, 0, owner, slot], local)
        shift = moveouts[j, m]
        whole = shift // LANES
        rest = shift % LANES
        first = local + whole * PAD
        low = lanes[k, pl.ds(first, reach, stride=PAD), :]
        up = lanes[k, pl.ds(first + PAD, reach, stride=PAD), :]
        back = (LANES - rest) % LANES
        low = pltpu.roll(low, back, axis=1)
        up = pltpu.roll(up, back, axis=1)
        stacks[p, :reach, :] = jnp.where(lane < LANES - rest, low, up)
        for d in range(depth // LANES):
            piece = stacks[p, d : d + groups, :]
            taps[p * groups : (p + 1) * groups, d * LANES : (d + 1) * LANES] = piece
            squares[p * groups : (p + 1) * groups, d * LANES : (d + 1) * LANES] = piece * piece
    contract = (((1,), (1,)), ((), ()))
    square = squares[...]
    main = square.astype(jnp.bfloat16)
    left = (square - main.astype(jnp.float32)).astype(jnp.bfloat16)
    energy = lax.dot_general(main, box[...], contract, preferred_element_type=jnp.float32)
    energy += lax.dot_general(left, box[...], contract, preferred_element_type=jnp.float32)
    norm = scale[...] * lax.rsqrt(energy * (1.0 / tlen) + EPS)
    product = lax.dot_general(taps[...].astype(jnp.bfloat16), bands[...], contract, preferred_element_type=jnp.float32)
    for m in range(count):
        partial = jnp.zeros((groups, LANES), jnp.float32)
        total = jnp.int32(0)
        for j in range(slots):
            p = m * slots + j
            rows = slice(p * groups, (p + 1) * groups)
            partial += product[rows, p * LANES : (p + 1) * LANES] * norm[rows, :]
            total += weights[j, m] * weights[j, m]
        stacked = jnp.broadcast_to(total.astype(jnp.float32), (groups, LANES))
        blocks[:, m, :] = partial
        blocks[:, count + m, :] = stacked
    width = LAGS // columns
    if width == LANES:
        for k in range(columns):
            outs[k][...] = blocks[column ^ k]
    else:
        share = LANES // width
        for k in range(columns):
            target = column ^ k
            part = blocks[target // share]
            chosen = part[:, :width]
            for s in range(1, share):
                chosen = jnp.where(target % share == s, part[:, s * width : (s + 1) * width], chosen)
            outs[k][...] = chosen


def shards(waveforms, templates, selection, channel_list, moveouts, weights):
    owners = lax.axis_size("tmpl")
    columns = lax.axis_size("chan")
    capacity = selection.shape[3]
    count, slots, tlen = templates.shape
    pairs = count * slots
    groups = LAGS // LANES
    depth = -(-(tlen + LANES - 1) // LANES) * LANES
    pieces = waveforms.shape[1] // LANES
    smem = pl.BlockSpec(memory_space=pltpu.SMEM)
    vmem = pl.BlockSpec(memory_space=pltpu.VMEM)
    lists, offsets, factors = channel_list.T, moveouts.T, weights.T
    records, selections = [waveforms], [selection]
    distance = owners // 2
    reached = [0]
    while distance:
        records += [exchange(r, "tmpl", distance) for r in records]
        selections += [exchange(s, "tmpl", distance) for s in selections]
        reached += [k ^ distance for k in reached]
        distance //= 2
    order = [reached.index(k) for k in range(owners)]
    records = [records[i] for i in order]
    selections = [selections[i] for i in order]
    bands, box, scale = pl.pallas_call(
        functools.partial(prepare, tlen),
        out_shape=(
            jax.ShapeDtypeStruct((pairs * LANES, depth), jnp.bfloat16),
            jax.ShapeDtypeStruct((LANES, depth), jnp.bfloat16),
            jax.ShapeDtypeStruct((pairs * groups, LANES), jnp.float32),
        ),
        in_specs=[vmem, smem],
        out_specs=(vmem, vmem, vmem),
        scratch_shapes=[pltpu.VMEM((pairs, depth), jnp.float32)],
        name="prepare",
    )(templates, factors)
    spot = jnp.stack([lax.axis_index("tmpl"), lax.axis_index("chan")]).astype(jnp.int32)
    parts = pl.pallas_call(
        functools.partial(correlate, owners, columns, tlen, capacity),
        out_shape=tuple(jax.ShapeDtypeStruct((2 * count, LAGS // columns), jnp.float32) for _ in range(columns)),
        in_specs=[smem] * (4 + owners) + [vmem] * (owners + 3),
        out_specs=(vmem,) * columns,
        scratch_shapes=[
            pltpu.VMEM((owners, (pieces + 2) * PAD, LANES), jnp.float32),
            pltpu.VMEM((pairs * groups, depth), jnp.float32),
            pltpu.VMEM((pairs * groups, depth), jnp.float32),
            pltpu.VMEM((pairs, PAD, LANES), jnp.float32),
            pltpu.VMEM((groups, 2 * count, LANES), jnp.float32),
        ],
        name="correlate",
    )(spot, lists, offsets, factors, *selections, *records, bands, box, scale)
    parts = list(parts)
    distance = 1
    while distance < columns:
        kept = range(0, columns, 2 * distance)
        arrived = {k: exchange(parts[k + distance], "chan", distance) for k in kept}
        for k in kept:
            parts[k] = parts[k] + arrived[k]
        distance *= 2
    return parts[0][:count] / jnp.sqrt(parts[0][count:])


def solution(mesh):
    placed = (
        P(("parts", "tmpl", "chan"), None),
        P(("parts", "tmpl"), "chan", None),
        P(("parts", "tmpl"), "chan", None, None),
        P(("parts", "tmpl"), "chan"),
        P(("parts", "tmpl"), "chan"),
        P(("parts", "tmpl"), "chan"),
    )
    return jax.shard_map(
        shards, mesh=mesh, in_specs=placed, out_specs=P(("parts", "tmpl"), "chan"), check_vma=False
    )
```

```python
import functools

import jax
import jax.numpy as jnp
from jax import lax
from jax.experimental import pallas as pl
from jax.experimental.pallas import tpu as pltpu
from jax.sharding import PartitionSpec as P

LAGS = 512
EPS = 1e-06
LANES = 128
PAD = 16
PARAMS = pltpu.CompilerParams(vmem_limit_bytes=8 * 1024 * 1024)
NT = (((1,), (1,)), ((), ()))
VMEM = pl.BlockSpec(memory_space=pltpu.VMEM)
HBM = pl.BlockSpec(memory_space=pltpu.HBM)


def exchange(value, axis, distance):
    size = lax.axis_size(axis)
    return lax.ppermute(value, axis, [(i, i ^ distance) for i in range(size)])


def fetch(sources, targets, sems):
    copies = [pltpu.make_async_copy(a, b, sems.at[i]) for i, (a, b) in enumerate(zip(sources, targets))]
    for copy in copies:
        copy.start()
    return copies


def pack(waveforms, selection, packed, taken, choice, sems):
    high, samples = waveforms.shape
    _, _, owners, capacity = choice.shape
    for copy in fetch((waveforms, selection), (taken, choice), sems):
        copy.wait()
    notes = choice[0, 0].astype(jnp.float32)
    notes = jnp.pad(notes, ((0, packed.shape[0] - high - owners), (0, samples - capacity)))
    packed[...] = jnp.concatenate([taken[...].astype(jnp.float32), notes], axis=0).astype(jnp.bfloat16)


def prepare(
    tlen, templates, lists, moveouts, weights, bands, box, scale, totals, table, rows, taken, entries, shifts, factors, sems
):
    copies = fetch((templates, lists, moveouts, weights), (taken, entries, shifts, factors), sems)
    count, slots, _ = taken.shape
    pairs = count * slots
    depth = box.shape[1]
    groups = LAGS // LANES
    tap = lax.broadcasted_iota(jnp.int32, (LANES, depth), 1) - lax.broadcasted_iota(jnp.int32, (LANES, depth), 0)
    box[...] = jnp.where((tap >= 0) & (tap < tlen), 1.0, 0.0).astype(jnp.bfloat16)
    rows[...] = jnp.zeros_like(rows)
    for copy in copies:
        copy.wait()
    for m in range(count):
        rows[m * slots : (m + 1) * slots, :tlen] = taken[m].astype(jnp.float32)
    row = lax.broadcasted_iota(jnp.int32, (LANES, LANES), 0)
    lane = lax.broadcasted_iota(jnp.int32, (LANES, LANES), 1)
    late = lane >= row
    zero = jnp.zeros((LANES, LANES), jnp.float32)
    values = rows[...]
    power = jnp.sum(values * values, axis=1, keepdims=True) / tlen
    factor = 1.0 / (jnp.sqrt(jnp.float32(tlen)) * jnp.sqrt(power + EPS))
    for p in range(pairs):
        m, j = p // slots, p % slots
        table[p : p + 1, :] = jnp.full((1, LANES), entries[j, m])
        table[pairs + p : pairs + p + 1, :] = jnp.full((1, LANES), shifts[j, m])
        weight = factors[j, m].astype(jnp.float32)
        scale[p * groups : (p + 1) * groups, :] = jnp.broadcast_to(factor[p : p + 1] * weight, (groups, LANES))
        before = zero
        for d in range(depth // LANES):
            if d * LANES < tlen:
                part = jnp.broadcast_to(rows[p : p + 1, d * LANES : (d + 1) * LANES], (LANES, LANES))
                now = pltpu.roll(part, 0, axis=1, stride=1, stride_axis=0)
            else:
                now = zero
            bands[p * LANES : (p + 1) * LANES, d * LANES : (d + 1) * LANES] = jnp.where(late, now, before).astype(jnp.bfloat16)
            before = now
    for m in range(count):
        total = jnp.int32(0)
        for j in range(slots):
            total += factors[j, m] * factors[j, m]
        totals[m : m + 1, :] = jnp.full((1, LANES), total.astype(jnp.float32))


def correlate(owners, columns, tlen, high, capacity, count, slots, table, *refs):
    packed, refs = refs[:owners], refs[owners:]
    bands, box, scale, totals = refs[:4]
    outs, (gathered, lanes, taps, squares, stacks, blocks) = refs[4:-6], refs[-6:]
    owner, column = lax.axis_index("tmpl"), lax.axis_index("chan")
    pairs = count * slots
    depth = box.shape[1]
    tall, samples = packed[0].shape
    pieces = samples // LANES
    groups = LAGS // LANES
    reach = groups + depth // LANES - 1
    spot = lax.broadcasted_iota(jnp.int32, (pairs, LANES), 1)
    entry = table[:pairs, :]
    shifts = table[pairs:, :]
    mark = lax.broadcasted_iota(jnp.int32, (tall, LANES), 0) == high + owner
    found = jnp.zeros((pairs, LANES), jnp.float32)
    for k in range(owners):
        local = jnp.sum(jnp.where(mark, packed[k][:, :LANES].astype(jnp.float32), 0.0), axis=0, keepdims=True)
        start = (owner ^ k) * capacity
        found = jnp.where((entry == start + spot) & (spot < capacity), local + float(k * PAD), found)
        gathered[k * PAD : (k + 1) * PAD, :] = packed[k][:PAD, :]
    index = jnp.sum(found, axis=1, keepdims=True).astype(jnp.int32)
    picks = jnp.where(lax.broadcasted_iota(jnp.int32, (pairs, owners * PAD), 1) == index, 1.0, 0.0).astype(jnp.bfloat16)
    picked = jnp.dot(picks, gathered[...], preferred_element_type=jnp.float32)
    for d in range(pieces):
        lanes[d * pairs : (d + 1) * pairs, :] = picked[:, d * LANES : (d + 1) * LANES]
    lanes[pieces * pairs :, :] = jnp.zeros((lanes.shape[0] - pieces * pairs, LANES), jnp.float32)
    lane = lax.broadcasted_iota(jnp.int32, (reach, LANES), 1)
    for p in range(pairs):
        shift = shifts[p, 0]
        rest = shift % LANES
        first = p + (shift // LANES) * pairs
        back = (LANES - rest) % LANES
        low = pltpu.roll(lanes[pl.ds(first, reach, stride=pairs), :], back, axis=1)
        up = pltpu.roll(lanes[pl.ds(first + pairs, reach, stride=pairs), :], back, axis=1)
        stacks[p, :reach, :] = jnp.where(lane < LANES - rest, low, up)
        for d in range(depth // LANES):
            piece = stacks[p, d : d + groups, :]
            taps[p * groups : (p + 1) * groups, d * LANES : (d + 1) * LANES] = piece
            squares[p * groups : (p + 1) * groups, d * LANES : (d + 1) * LANES] = piece * piece
    square = squares[...]
    main = square.astype(jnp.bfloat16)
    left = (square - main.astype(jnp.float32)).astype(jnp.bfloat16)
    energy = lax.dot_general(main, box[...], NT, preferred_element_type=jnp.float32)
    energy += lax.dot_general(left, box[...], NT, preferred_element_type=jnp.float32)
    norm = scale[...] * lax.rsqrt(energy * (1.0 / tlen) + EPS)
    product = lax.dot_general(taps[...].astype(jnp.bfloat16), bands[...], NT, preferred_element_type=jnp.float32)
    for m in range(count):
        partial = jnp.zeros((groups, LANES), jnp.float32)
        for j in range(slots):
            p = m * slots + j
            rows = slice(p * groups, (p + 1) * groups)
            partial += product[rows, p * LANES : (p + 1) * LANES] * norm[rows, :]
        blocks[:, m, :] = partial
        blocks[:, count + m, :] = jnp.broadcast_to(totals[m : m + 1, :], (groups, LANES))
    width = LAGS // columns
    share = LANES // width

    def block(target):
        part = blocks[target // share]
        chosen = part[:, :width]
        for s in range(1, share):
            chosen = jnp.where(target % share == s, part[:, s * width : (s + 1) * width], chosen)
        return chosen

    outs[-1][...] = block(column)
    distance = 1
    for out in outs[:-1]:
        for q in range(out.shape[0]):
            out[q] = block(column ^ (distance * (2 * q + 1)))
        distance *= 2


def shards(waveforms, templates, selection, channel_list, moveouts, weights):
    owners = lax.axis_size("tmpl")
    columns = lax.axis_size("chan")
    count, slots, tlen = templates.shape
    pairs = count * slots
    groups = LAGS // LANES
    width = LAGS // columns
    high, samples = waveforms.shape
    capacity = selection.shape[3]
    depth = -(-(tlen + LANES - 1) // LANES) * LANES
    pieces = samples // LANES

    def call(kernel, name, ins, outs, scratch, arguments, cost=None):
        if ins is HBM:
            arguments = [pltpu.with_memory_space_constraint(x, pltpu.HBM) for x in arguments]
        single = not isinstance(outs, tuple)
        return pl.pallas_call(
            kernel,
            out_shape=outs,
            in_specs=[ins] * len(arguments),
            out_specs=VMEM if single else (VMEM,) * len(outs),
            scratch_shapes=scratch,
            compiler_params=PARAMS,
            cost_estimate=cost,
            name=name,
        )(*arguments)

    bundle = call(
        pack,
        "pack",
        HBM,
        jax.ShapeDtypeStruct((-(-(high + owners) // PAD) * PAD, samples), waveforms.dtype),
        [
            pltpu.VMEM(waveforms.shape, waveforms.dtype),
            pltpu.VMEM(selection.shape, selection.dtype),
            pltpu.SemaphoreType.DMA((2,)),
        ],
        (waveforms, selection),
    )
    packed, reached = [bundle], [0]
    distance = owners // 2
    while distance:
        packed += [exchange(x, "tmpl", distance) for x in packed]
        reached += [k ^ distance for k in reached]
        distance //= 2
    packed = [packed[reached.index(k)] for k in range(owners)]
    bands, box, scale, totals, table = call(
        functools.partial(prepare, tlen),
        "prepare",
        HBM,
        (
            jax.ShapeDtypeStruct((pairs * LANES, depth), jnp.bfloat16),
            jax.ShapeDtypeStruct((LANES, depth), jnp.bfloat16),
            jax.ShapeDtypeStruct((pairs * groups, LANES), jnp.float32),
            jax.ShapeDtypeStruct((count, LANES), jnp.float32),
            jax.ShapeDtypeStruct((2 * pairs, LANES), jnp.int32),
        ),
        [
            pltpu.VMEM((pairs, depth), jnp.float32),
            pltpu.VMEM(templates.shape, templates.dtype),
            pltpu.SMEM((slots, count), jnp.int32),
            pltpu.SMEM((slots, count), jnp.int32),
            pltpu.SMEM((slots, count), jnp.int32),
            pltpu.SemaphoreType.DMA((4,)),
        ],
        (templates, channel_list.T, moveouts.T, weights.T),
        pl.CostEstimate(flops=2_000_000, bytes_accessed=2_000_000, transcendentals=0),
    )
    sizes = []
    while (columns >> len(sizes)) > 1:
        sizes.append(columns >> (len(sizes) + 1))
    shapes = [(s, 2 * count, width) for s in sizes] + [(2 * count, width)]
    parts = call(
        functools.partial(correlate, owners, columns, tlen, high, capacity, count, slots),
        "correlate",
        VMEM,
        tuple(jax.ShapeDtypeStruct(s, jnp.float32) for s in shapes),
        [
            pltpu.VMEM((owners * PAD, samples), jnp.bfloat16),
            pltpu.VMEM(((pieces + 2) * pairs, LANES), jnp.float32),
            pltpu.VMEM((pairs * groups, depth), jnp.float32),
            pltpu.VMEM((pairs * groups, depth), jnp.float32),
            pltpu.VMEM((pairs, PAD, LANES), jnp.float32),
            pltpu.VMEM((groups, 2 * count, LANES), jnp.float32),
        ],
        (table, *packed, bands, box, scale, totals),
    )
    stages, own = list(parts[:-1]), [parts[-1]]
    for i in range(len(stages)):
        arrived = exchange(stages[i], "chan", 1 << i)
        own.append(arrived[0])
        for later in range(i + 1, len(stages)):
            step = 1 << (later - i)
            stages[later] = stages[later] + arrived[step // 2 :: step]
    top = sum(x[:count] for x in own)
    return top / jnp.sqrt(sum(x[count:] for x in own))


def solution(mesh):
    placed = (
        P(("parts", "tmpl", "chan"), None),
        P(("parts", "tmpl"), "chan", None),
        P(("parts", "tmpl"), "chan", None, None),
        P(("parts", "tmpl"), "chan"),
        P(("parts", "tmpl"), "chan"),
        P(("parts", "tmpl"), "chan"),
    )
    return jax.shard_map(
        shards, mesh=mesh, in_specs=placed, out_specs=P(("parts", "tmpl"), "chan"), check_vma=False
    )
```

```python
import functools

import jax
import jax.numpy as jnp
from jax import lax
from jax.experimental import pallas as pl
from jax.experimental.pallas import tpu as pltpu
from jax.sharding import PartitionSpec as P

LAGS = 512
EPS = 1e-06
LANES = 128
PAD = 16
PARAMS = pltpu.CompilerParams(vmem_limit_bytes=8 * 1024 * 1024)
STEP = 64
VMEM = pl.BlockSpec(memory_space=pltpu.VMEM)
HBM = pl.BlockSpec(memory_space=pltpu.HBM)


def exchange(value, axis, distance):
    size = lax.axis_size(axis)
    return lax.ppermute(value, axis, [(i, i ^ distance) for i in range(size)])


def fetch(sources, targets, sems):
    copies = [pltpu.make_async_copy(a, b, sems.at[i]) for i, (a, b) in enumerate(zip(sources, targets))]
    for copy in copies:
        copy.start()
    return copies


def pack(waveforms, selection, packed, taken, choice, sems):
    high, samples = waveforms.shape
    _, _, owners, capacity = choice.shape
    for copy in fetch((waveforms, selection), (taken, choice), sems):
        copy.wait()
    notes = choice[0, 0].astype(jnp.float32)
    notes = jnp.pad(notes, ((0, packed.shape[0] - high - owners), (0, samples - capacity)))
    packed[...] = jnp.concatenate([taken[...].astype(jnp.float32), notes], axis=0).astype(jnp.bfloat16)


def prepare(
    tlen, templates, lists, moveouts, weights, bands, box, scale, totals, table, rows, taken, entries, shifts, factors, sems
):
    copies = fetch((templates, lists, moveouts, weights), (taken, entries, shifts, factors), sems)
    count, slots, _ = taken.shape
    pairs = count * slots
    depth = box.shape[0]
    groups = LAGS // STEP
    tap = lax.broadcasted_iota(jnp.int32, (depth, LANES), 0) - lax.broadcasted_iota(jnp.int32, (depth, LANES), 1) % STEP
    box[...] = jnp.where((tap >= 0) & (tap < tlen), 1.0, 0.0).astype(jnp.bfloat16)
    rows[...] = jnp.zeros_like(rows)
    for copy in copies:
        copy.wait()
    for m in range(count):
        rows[m * slots : (m + 1) * slots, :tlen] = taken[m].astype(jnp.float32)
    row = lax.broadcasted_iota(jnp.int32, (LANES, LANES), 0)
    lane = lax.broadcasted_iota(jnp.int32, (LANES, LANES), 1)
    late = row >= lane % STEP
    front = lane < STEP
    mirror = jnp.where(row + lane == LANES - 1, 1.0, 0.0).astype(jnp.bfloat16)
    zero = jnp.zeros((LANES, LANES), jnp.float32)
    values = rows[...]
    power = jnp.sum(values * values, axis=1, keepdims=True) / tlen
    factor = 1.0 / (jnp.sqrt(jnp.float32(tlen)) * jnp.sqrt(power + EPS))
    for p in range(pairs):
        m, j = p // slots, p % slots
        table[p : p + 1, :] = jnp.full((1, LANES), entries[j, m])
        table[pairs + p : pairs + p + 1, :] = jnp.full((1, LANES), shifts[j, m])
        weight = factors[j, m].astype(jnp.float32)
        scale[p * groups : (p + 1) * groups, :] = jnp.broadcast_to(factor[p : p + 1] * weight, (groups, LANES))
    turned = [
        jnp.dot(values[:, d * LANES : (d + 1) * LANES].astype(jnp.bfloat16), mirror, preferred_element_type=jnp.float32)
        for d in range(-(-tlen // LANES))
    ]
    for m in range(count):
        before = zero
        for d in range(depth // LANES):
            now = zero
            if d * LANES < tlen:
                back = turned[d][m * slots : (m + 1) * slots, :]
                now, other = (
                    pltpu.roll(jnp.broadcast_to(back[j : j + 1], (LANES, LANES)), 1 + j * STEP, axis=1, stride=1, stride_axis=0)
                    for j in range(slots)
                )
                now = jnp.where(front, now, other)
            bands[d * LANES : (d + 1) * LANES, m * LANES : (m + 1) * LANES] = jnp.where(late, now, before).astype(jnp.bfloat16)
            before = now
        total = jnp.int32(0)
        for j in range(slots):
            total += factors[j, m] * factors[j, m]
        totals[m : m + 1, :] = jnp.full((1, LANES), total.astype(jnp.float32))


def correlate(owners, columns, tlen, high, capacity, count, slots, table, *refs):
    packed, refs = refs[:owners], refs[owners:]
    bands, box, scale, totals = refs[:4]
    outs, (gathered, lanes, taps, squares, stacks, sums, blocks) = refs[4:-7], refs[-7:]
    owner, column = lax.axis_index("tmpl"), lax.axis_index("chan")
    pairs = count * slots
    depth = box.shape[0]
    tall, samples = packed[0].shape
    pieces = samples // LANES
    groups = LAGS // STEP
    turns = LANES // STEP
    reach = LAGS // LANES + depth // LANES - 1
    spot = lax.broadcasted_iota(jnp.int32, (pairs, LANES), 1)
    entry = table[:pairs, :]
    shifts = table[pairs:, :]
    mark = lax.broadcasted_iota(jnp.int32, (tall, LANES), 0) == high + owner
    found = jnp.zeros((pairs, LANES), jnp.float32)
    for k in range(owners):
        local = jnp.sum(jnp.where(mark, packed[k][:, :LANES].astype(jnp.float32), 0.0), axis=0, keepdims=True)
        start = (owner ^ k) * capacity
        found = jnp.where((entry == start + spot) & (spot < capacity), local + float(k * PAD), found)
        gathered[k * PAD : (k + 1) * PAD, :] = packed[k][:PAD, :]
    index = jnp.sum(found, axis=1, keepdims=True).astype(jnp.int32)
    picks = jnp.where(lax.broadcasted_iota(jnp.int32, (pairs, owners * PAD), 1) == index, 1.0, 0.0).astype(jnp.bfloat16)
    picked = jnp.dot(picks, gathered[...], preferred_element_type=jnp.float32)
    for d in range(pieces):
        lanes[d * pairs : (d + 1) * pairs, :] = picked[:, d * LANES : (d + 1) * LANES]
    lanes[pieces * pairs :, :] = jnp.zeros((lanes.shape[0] - pieces * pairs, LANES), jnp.float32)
    lane = lax.broadcasted_iota(jnp.int32, (reach, LANES), 1)
    for p in range(pairs):
        for h in range(turns):
            shift = shifts[p, 0] + h * STEP
            rest = shift % LANES
            first = p + (shift // LANES) * pairs
            back = (LANES - rest) % LANES
            low = pltpu.roll(lanes[pl.ds(first, reach, stride=pairs), :], back, axis=1)
            up = pltpu.roll(lanes[pl.ds(first + pairs, reach, stride=pairs), :], back, axis=1)
            stacks[p, pl.ds(h, reach, stride=turns), :] = jnp.where(lane < LANES - rest, low, up)
        for d in range(depth // LANES):
            piece = stacks[p, d * turns : d * turns + groups, :]
            taps[p * groups : (p + 1) * groups, d * LANES : (d + 1) * LANES] = piece
            squares[p * groups : (p + 1) * groups, d * LANES : (d + 1) * LANES] = piece * piece
    square = squares[...]
    main = square.astype(jnp.bfloat16)
    left = (square - main.astype(jnp.float32)).astype(jnp.bfloat16)
    energy = jnp.dot(main, box[...], preferred_element_type=jnp.float32)
    energy += jnp.dot(left, box[...], preferred_element_type=jnp.float32)
    norm = scale[...] * lax.rsqrt(energy * (1.0 / tlen) + EPS)
    product = jnp.dot(taps[...].astype(jnp.bfloat16), bands[...], preferred_element_type=jnp.float32)
    front = lax.broadcasted_iota(jnp.int32, (LAGS // LANES, LANES), 1) < STEP
    for m in range(count):
        first, second = (slice((m * slots + j) * groups, (m * slots + j + 1) * groups) for j in range(slots))
        place = slice(m * LANES, (m + 1) * LANES)
        sums[m] = product[first, place] * norm[first, :] + pltpu.roll(product[second, place] * norm[second, :], STEP, axis=1)
        even = sums[m, pl.ds(0, LAGS // LANES, stride=turns), :]
        odd = sums[m, pl.ds(1, LAGS // LANES, stride=turns), :]
        blocks[:, m, :] = jnp.where(front, even, pltpu.roll(odd, STEP, axis=1))
        blocks[:, count + m, :] = jnp.broadcast_to(totals[m : m + 1, :], (LAGS // LANES, LANES))
    width = LAGS // columns
    share = LANES // width

    def block(target):
        part = blocks[target // share]
        chosen = part[:, :width]
        for s in range(1, share):
            chosen = jnp.where(target % share == s, part[:, s * width : (s + 1) * width], chosen)
        return chosen

    outs[-1][...] = block(column)
    distance = 1
    for out in outs[:-1]:
        for q in range(out.shape[0]):
            out[q] = block(column ^ (distance * (2 * q + 1)))
        distance *= 2


def shards(waveforms, templates, selection, channel_list, moveouts, weights):
    owners = lax.axis_size("tmpl")
    columns = lax.axis_size("chan")
    count, slots, tlen = templates.shape
    pairs = count * slots
    groups = LAGS // STEP
    width = LAGS // columns
    high, samples = waveforms.shape
    capacity = selection.shape[3]
    depth = -(-(tlen + STEP - 1) // LANES) * LANES
    pieces = samples // LANES

    def call(kernel, name, ins, outs, scratch, arguments, cost=None):
        if ins is HBM:
            arguments = [pltpu.with_memory_space_constraint(x, pltpu.HBM) for x in arguments]
        single = not isinstance(outs, tuple)
        return pl.pallas_call(
            kernel,
            out_shape=outs,
            in_specs=[ins] * len(arguments),
            out_specs=VMEM if single else (VMEM,) * len(outs),
            scratch_shapes=scratch,
            compiler_params=PARAMS,
            cost_estimate=cost,
            name=name,
        )(*arguments)

    bundle = call(
        pack,
        "pack",
        HBM,
        jax.ShapeDtypeStruct((-(-(high + owners) // PAD) * PAD, samples), waveforms.dtype),
        [
            pltpu.VMEM(waveforms.shape, waveforms.dtype),
            pltpu.VMEM(selection.shape, selection.dtype),
            pltpu.SemaphoreType.DMA((2,)),
        ],
        (waveforms, selection),
    )
    bands, box, scale, totals, table = call(
        functools.partial(prepare, tlen),
        "prepare",
        HBM,
        (
            jax.ShapeDtypeStruct((depth, pairs * STEP), jnp.bfloat16),
            jax.ShapeDtypeStruct((depth, LANES), jnp.bfloat16),
            jax.ShapeDtypeStruct((pairs * groups, LANES), jnp.float32),
            jax.ShapeDtypeStruct((count, LANES), jnp.float32),
            jax.ShapeDtypeStruct((2 * pairs, LANES), jnp.int32),
        ),
        [
            pltpu.VMEM((pairs, depth), jnp.float32),
            pltpu.VMEM(templates.shape, templates.dtype),
            pltpu.SMEM((slots, count), jnp.int32),
            pltpu.SMEM((slots, count), jnp.int32),
            pltpu.SMEM((slots, count), jnp.int32),
            pltpu.SemaphoreType.DMA((4,)),
        ],
        (templates, channel_list.T, moveouts.T, weights.T),
        pl.CostEstimate(flops=2_000_000, bytes_accessed=2_000_000, transcendentals=0),
    )
    packed, reached = [bundle], [0]
    distance = owners // 2
    while distance:
        packed += [exchange(x, "tmpl", distance) for x in packed]
        if distance == owners // 2:
            packed[1], table = lax.optimization_barrier((packed[1], table))
        reached += [k ^ distance for k in reached]
        distance //= 2
    packed = [packed[reached.index(k)] for k in range(owners)]
    sizes = []
    while (columns >> len(sizes)) > 1:
        sizes.append(columns >> (len(sizes) + 1))
    shapes = [(s, 2 * count, width) for s in sizes] + [(2 * count, width)]
    parts = call(
        functools.partial(correlate, owners, columns, tlen, high, capacity, count, slots),
        "correlate",
        VMEM,
        tuple(jax.ShapeDtypeStruct(s, jnp.float32) for s in shapes),
        [
            pltpu.VMEM((owners * PAD, samples), jnp.bfloat16),
            pltpu.VMEM(((pieces + 2) * pairs, LANES), jnp.float32),
            pltpu.VMEM((pairs * groups, depth), jnp.float32),
            pltpu.VMEM((pairs * groups, depth), jnp.float32),
            pltpu.VMEM((pairs, 2 * PAD, LANES), jnp.float32),
            pltpu.VMEM((count, groups, LANES), jnp.float32),
            pltpu.VMEM((LAGS // LANES, 2 * count, LANES), jnp.float32),
        ],
        (table, *packed, bands, box, scale, totals),
    )
    stages, own = list(parts[:-1]), [parts[-1]]
    for i in range(len(stages)):
        arrived = exchange(stages[i], "chan", 1 << i)
        own.append(arrived[0])
        for later in range(i + 1, len(stages)):
            step = 1 << (later - i)
            stages[later] = stages[later] + arrived[step // 2 :: step]
    top = sum(x[:count] for x in own)
    return top / jnp.sqrt(sum(x[count:] for x in own))


def solution(mesh):
    placed = (
        P(("parts", "tmpl", "chan"), None),
        P(("parts", "tmpl"), "chan", None),
        P(("parts", "tmpl"), "chan", None, None),
        P(("parts", "tmpl"), "chan"),
        P(("parts", "tmpl"), "chan"),
        P(("parts", "tmpl"), "chan"),
    )
    return jax.shard_map(
        shards, mesh=mesh, in_specs=placed, out_specs=P(("parts", "tmpl"), "chan"), check_vma=False
    )
```

```python
import functools

import jax
import jax.numpy as jnp
from jax import lax
from jax.experimental import pallas as pl
from jax.experimental.pallas import tpu as pltpu
from jax.sharding import PartitionSpec as P

LAGS = 512
EPS = 1e-06
LANES = 128
PAD = 16
PARAMS = pltpu.CompilerParams(vmem_limit_bytes=8 * 1024 * 1024)
STEP = 64
ROUTES = {4: ((2, 3, 1, 0), (3, 2, 0, 1), (1, 0, 3, 2))}
VMEM = pl.BlockSpec(memory_space=pltpu.VMEM)
HBM = pl.BlockSpec(memory_space=pltpu.HBM)


def exchange(value, axis, distance):
    size = lax.axis_size(axis)
    return lax.ppermute(value, axis, [(i, i ^ distance) for i in range(size)])


def fetch(sources, targets, sems):
    copies = [pltpu.make_async_copy(a, b, sems.at[i]) for i, (a, b) in enumerate(zip(sources, targets))]
    for copy in copies:
        copy.start()
    return copies


def pack(waveforms, selection, packed, taken, choice, sems):
    high, samples = waveforms.shape
    _, _, owners, capacity = choice.shape
    for copy in fetch((waveforms, selection), (taken, choice), sems):
        copy.wait()
    notes = choice[0, 0].astype(jnp.float32)
    notes = jnp.pad(notes, ((0, packed.shape[0] - high - owners), (0, samples - capacity)))
    packed[...] = jnp.concatenate([taken[...].astype(jnp.float32), notes], axis=0).astype(jnp.bfloat16)


def prepare(
    tlen, templates, lists, moveouts, weights, bands, box, scale, totals, table, rows, taken, entries, shifts, factors, sems
):
    copies = fetch((templates, lists, moveouts, weights), (taken, entries, shifts, factors), sems)
    count, slots, _ = taken.shape
    pairs = count * slots
    depth = box.shape[0]
    groups = LAGS // STEP
    tap = lax.broadcasted_iota(jnp.int32, (depth, LANES), 0) - lax.broadcasted_iota(jnp.int32, (depth, LANES), 1) % STEP
    box[...] = jnp.where((tap >= 0) & (tap < tlen), 1.0, 0.0).astype(jnp.bfloat16)
    rows[...] = jnp.zeros_like(rows)
    for copy in copies:
        copy.wait()
    for m in range(count):
        rows[m * slots : (m + 1) * slots, :tlen] = taken[m].astype(jnp.float32)
    row = lax.broadcasted_iota(jnp.int32, (LANES, LANES), 0)
    lane = lax.broadcasted_iota(jnp.int32, (LANES, LANES), 1)
    late = row >= lane % STEP
    front = lane < STEP
    mirror = jnp.where(row + lane == LANES - 1, 1.0, 0.0).astype(jnp.bfloat16)
    zero = jnp.zeros((LANES, LANES), jnp.float32)
    values = rows[...]
    power = jnp.sum(values * values, axis=1, keepdims=True) / tlen
    factor = 1.0 / (jnp.sqrt(jnp.float32(tlen)) * jnp.sqrt(power + EPS))
    for p in range(pairs):
        m, j = p // slots, p % slots
        table[p : p + 1, :] = jnp.full((1, LANES), entries[j, m])
        table[pairs + p : pairs + p + 1, :] = jnp.full((1, LANES), shifts[j, m])
        weight = factors[j, m].astype(jnp.float32)
        scale[p * groups : (p + 1) * groups, :] = jnp.broadcast_to(factor[p : p + 1] * weight, (groups, LANES))
    turned = [
        jnp.dot(values[:, d * LANES : (d + 1) * LANES].astype(jnp.bfloat16), mirror, preferred_element_type=jnp.float32)
        for d in range(-(-tlen // LANES))
    ]
    for m in range(count):
        before = zero
        for d in range(depth // LANES):
            now = zero
            if d * LANES < tlen:
                back = turned[d][m * slots : (m + 1) * slots, :]
                now, other = (
                    pltpu.roll(jnp.broadcast_to(back[j : j + 1], (LANES, LANES)), 1 + j * STEP, axis=1, stride=1, stride_axis=0)
                    for j in range(slots)
                )
                now = jnp.where(front, now, other)
            bands[d * LANES : (d + 1) * LANES, m * LANES : (m + 1) * LANES] = jnp.where(late, now, before).astype(jnp.bfloat16)
            before = now
        total = jnp.int32(0)
        for j in range(slots):
            total += factors[j, m] * factors[j, m]
        totals[m : m + 1, :] = jnp.full((1, LANES), total.astype(jnp.float32))


def correlate(owners, columns, tlen, high, capacity, count, slots, table, *refs):
    packed, refs = refs[:owners], refs[owners:]
    bands, box, scale, totals = refs[:4]
    outs, (gathered, lanes, taps, squares, stacks, sums, blocks) = refs[4:-7], refs[-7:]
    owner, column = lax.axis_index("tmpl"), lax.axis_index("chan")
    pairs = count * slots
    depth = box.shape[0]
    tall, samples = packed[0].shape
    pieces = samples // LANES
    groups = LAGS // STEP
    turns = LANES // STEP
    reach = LAGS // LANES + depth // LANES - 1
    spot = lax.broadcasted_iota(jnp.int32, (pairs, LANES), 1)
    entry = table[:pairs, :]
    shifts = table[pairs:, :]
    mark = lax.broadcasted_iota(jnp.int32, (tall, LANES), 0) == high + owner
    found = jnp.zeros((pairs, LANES), jnp.float32)
    for k in range(owners):
        local = jnp.sum(jnp.where(mark, packed[k][:, :LANES].astype(jnp.float32), 0.0), axis=0, keepdims=True)
        start = (owner ^ k) * capacity
        found = jnp.where((entry == start + spot) & (spot < capacity), local + float(k * PAD), found)
        gathered[k * PAD : (k + 1) * PAD, :] = packed[k][:PAD, :]
    index = jnp.sum(found, axis=1, keepdims=True).astype(jnp.int32)
    picks = jnp.where(lax.broadcasted_iota(jnp.int32, (pairs, owners * PAD), 1) == index, 1.0, 0.0).astype(jnp.bfloat16)
    picked = jnp.dot(picks, gathered[...], preferred_element_type=jnp.float32)
    for d in range(pieces):
        lanes[d * pairs : (d + 1) * pairs, :] = picked[:, d * LANES : (d + 1) * LANES]
    lanes[pieces * pairs :, :] = jnp.zeros((lanes.shape[0] - pieces * pairs, LANES), jnp.float32)
    lane = lax.broadcasted_iota(jnp.int32, (reach, LANES), 1)
    for p in range(pairs):
        for h in range(turns):
            shift = shifts[p, 0] + h * STEP
            rest = shift % LANES
            first = p + (shift // LANES) * pairs
            back = (LANES - rest) % LANES
            low = pltpu.roll(lanes[pl.ds(first, reach, stride=pairs), :], back, axis=1)
            up = pltpu.roll(lanes[pl.ds(first + pairs, reach, stride=pairs), :], back, axis=1)
            stacks[p, pl.ds(h, reach, stride=turns), :] = jnp.where(lane < LANES - rest, low, up)
        for d in range(depth // LANES):
            piece = stacks[p, d * turns : d * turns + groups, :]
            taps[p * groups : (p + 1) * groups, d * LANES : (d + 1) * LANES] = piece
            squares[p * groups : (p + 1) * groups, d * LANES : (d + 1) * LANES] = piece * piece
    square = squares[...]
    main = square.astype(jnp.bfloat16)
    left = (square - main.astype(jnp.float32)).astype(jnp.bfloat16)
    energy = jnp.dot(main, box[...], preferred_element_type=jnp.float32)
    energy += jnp.dot(left, box[...], preferred_element_type=jnp.float32)
    norm = scale[...] * lax.rsqrt(energy * (1.0 / tlen) + EPS)
    product = jnp.dot(taps[...].astype(jnp.bfloat16), bands[...], preferred_element_type=jnp.float32)
    front = lax.broadcasted_iota(jnp.int32, (LAGS // LANES, LANES), 1) < STEP
    for m in range(count):
        first, second = (slice((m * slots + j) * groups, (m * slots + j + 1) * groups) for j in range(slots))
        place = slice(m * LANES, (m + 1) * LANES)
        sums[m] = product[first, place] * norm[first, :] + pltpu.roll(product[second, place] * norm[second, :], STEP, axis=1)
        even = sums[m, pl.ds(0, LAGS // LANES, stride=turns), :]
        odd = sums[m, pl.ds(1, LAGS // LANES, stride=turns), :]
        blocks[:, m, :] = jnp.where(front, even, pltpu.roll(odd, STEP, axis=1))
        blocks[:, count + m, :] = jnp.broadcast_to(totals[m : m + 1, :], (LAGS // LANES, LANES))
    width = LAGS // columns
    share = LANES // width

    def block(target):
        part = blocks[target // share]
        chosen = part[:, :width]
        for s in range(1, share):
            chosen = jnp.where(target % share == s, part[:, s * width : (s + 1) * width], chosen)
        return chosen

    outs[-1][...] = block(column)
    if columns in ROUTES:
        for out, route in zip(outs, ROUTES[columns]):
            target = jnp.int32(route[0])
            for i in range(1, columns):
                target = jnp.where(column == i, route[i], target)
            out[...] = block(target)
        return
    distance = 1
    for out in outs[:-1]:
        for q in range(out.shape[0]):
            out[q] = block(column ^ (distance * (2 * q + 1)))
        distance *= 2


def shards(waveforms, templates, selection, channel_list, moveouts, weights):
    owners = lax.axis_size("tmpl")
    columns = lax.axis_size("chan")
    count, slots, tlen = templates.shape
    pairs = count * slots
    groups = LAGS // STEP
    width = LAGS // columns
    high, samples = waveforms.shape
    capacity = selection.shape[3]
    depth = -(-(tlen + STEP - 1) // LANES) * LANES
    pieces = samples // LANES

    def call(kernel, name, ins, outs, scratch, arguments, cost=None):
        if ins is HBM:
            arguments = [pltpu.with_memory_space_constraint(x, pltpu.HBM) for x in arguments]
        single = not isinstance(outs, tuple)
        return pl.pallas_call(
            kernel,
            out_shape=outs,
            in_specs=[ins] * len(arguments),
            out_specs=VMEM if single else (VMEM,) * len(outs),
            scratch_shapes=scratch,
            compiler_params=PARAMS,
            cost_estimate=cost,
            name=name,
        )(*arguments)

    bundle = call(
        pack,
        "pack",
        HBM,
        jax.ShapeDtypeStruct((-(-(high + owners) // PAD) * PAD, samples), waveforms.dtype),
        [
            pltpu.VMEM(waveforms.shape, waveforms.dtype),
            pltpu.VMEM(selection.shape, selection.dtype),
            pltpu.SemaphoreType.DMA((2,)),
        ],
        (waveforms, selection),
    )
    bands, box, scale, totals, table = call(
        functools.partial(prepare, tlen),
        "prepare",
        HBM,
        (
            jax.ShapeDtypeStruct((depth, pairs * STEP), jnp.bfloat16),
            jax.ShapeDtypeStruct((depth, LANES), jnp.bfloat16),
            jax.ShapeDtypeStruct((pairs * groups, LANES), jnp.float32),
            jax.ShapeDtypeStruct((count, LANES), jnp.float32),
            jax.ShapeDtypeStruct((2 * pairs, LANES), jnp.int32),
        ),
        [
            pltpu.VMEM((pairs, depth), jnp.float32),
            pltpu.VMEM(templates.shape, templates.dtype),
            pltpu.SMEM((slots, count), jnp.int32),
            pltpu.SMEM((slots, count), jnp.int32),
            pltpu.SMEM((slots, count), jnp.int32),
            pltpu.SemaphoreType.DMA((4,)),
        ],
        (templates, channel_list.T, moveouts.T, weights.T),
        pl.CostEstimate(flops=2_000_000, bytes_accessed=2_000_000, transcendentals=0),
    )
    packed, reached = [bundle], [0]
    distance = owners // 2
    while distance:
        packed += [exchange(x, "tmpl", distance) for x in packed]
        if distance == owners // 2:
            packed[1], table = lax.optimization_barrier((packed[1], table))
        reached += [k ^ distance for k in reached]
        distance //= 2
    packed = [packed[reached.index(k)] for k in range(owners)]
    sizes = []
    while (columns >> len(sizes)) > 1:
        sizes.append(columns >> (len(sizes) + 1))
    shapes = [(s, 2 * count, width) for s in sizes] + [(2 * count, width)]
    if columns in ROUTES:
        shapes = [(2 * count, width)] * columns
    parts = call(
        functools.partial(correlate, owners, columns, tlen, high, capacity, count, slots),
        "correlate",
        VMEM,
        tuple(jax.ShapeDtypeStruct(s, jnp.float32) for s in shapes),
        [
            pltpu.VMEM((owners * PAD, samples), jnp.bfloat16),
            pltpu.VMEM(((pieces + 2) * pairs, LANES), jnp.float32),
            pltpu.VMEM((pairs * groups, depth), jnp.float32),
            pltpu.VMEM((pairs * groups, depth), jnp.float32),
            pltpu.VMEM((pairs, 2 * PAD, LANES), jnp.float32),
            pltpu.VMEM((count, groups, LANES), jnp.float32),
            pltpu.VMEM((LAGS // LANES, 2 * count, LANES), jnp.float32),
        ],
        (table, *packed, bands, box, scale, totals),
    )
    stages, own = list(parts[:-1]), [parts[-1]]
    if columns in ROUTES:
        for part, route in zip(stages, ROUTES[columns]):
            own.append(lax.ppermute(part, "chan", list(enumerate(route))))
        stages = []
    for i in range(len(stages)):
        arrived = exchange(stages[i], "chan", 1 << i)
        own.append(arrived[0])
        for later in range(i + 1, len(stages)):
            step = 1 << (later - i)
            stages[later] = stages[later] + arrived[step // 2 :: step]
    top = sum(x[:count] for x in own)
    return top / jnp.sqrt(sum(x[count:] for x in own))


def solution(mesh):
    placed = (
        P(("parts", "tmpl", "chan"), None),
        P(("parts", "tmpl"), "chan", None),
        P(("parts", "tmpl"), "chan", None, None),
        P(("parts", "tmpl"), "chan"),
        P(("parts", "tmpl"), "chan"),
        P(("parts", "tmpl"), "chan"),
    )
    return jax.shard_map(
        shards, mesh=mesh, in_specs=placed, out_specs=P(("parts", "tmpl"), "chan"), check_vma=False
    )
```

```python
import functools

import jax
import jax.numpy as jnp
from jax import lax
from jax.experimental import pallas as pl
from jax.experimental.pallas import tpu as pltpu
from jax.sharding import PartitionSpec as P

LAGS = 512
EPS = 1e-06
LANES = 128
PARAMS = pltpu.CompilerParams(vmem_limit_bytes=8 * 1024 * 1024)
STEP = 64
ROUTES = {
    ("tmpl", 4): ((3, 2, 0, 1), (2, 3, 1, 0), (1, 0, 3, 2)),
    ("chan", 4): ((2, 3, 1, 0), (3, 2, 0, 1), (1, 0, 3, 2)),
}
ROWS = 8
VMEM = pl.BlockSpec(memory_space=pltpu.VMEM)
HBM = pl.BlockSpec(memory_space=pltpu.HBM)


def exchange(value, axis, distance):
    size = lax.axis_size(axis)
    return lax.ppermute(value, axis, [(i, i ^ distance) for i in range(size)])


def routes(axis, size):
    return ROUTES.get((axis, size), tuple(tuple(i ^ k for i in range(size)) for k in range(1, size)))


def send(value, axis, route):
    return lax.ppermute(value, axis, list(enumerate(route)))


def lookup(values, place):
    found = jnp.int32(values[0])
    for i in range(1, len(values)):
        found = jnp.where(place == i, values[i], found)
    return found


def fetch(sources, targets, sems):
    copies = [pltpu.make_async_copy(a, b, sems.at[i]) for i, (a, b) in enumerate(zip(sources, targets))]
    for copy in copies:
        copy.start()
    return copies


def pack(waveforms, selection, *refs):
    outs, (taken, choice, sems) = refs[:-3], refs[-3:]
    copies = fetch((waveforms, selection), (taken, choice), sems)
    high, samples = waveforms.shape
    _, _, owners, capacity = choice.shape
    me = lax.axis_index("tmpl")
    tall = -(-high // 16) * 16
    row = lax.broadcasted_iota(jnp.int32, (ROWS, tall), 0)
    column = lax.broadcasted_iota(jnp.int32, (ROWS, tall), 1)
    for copy in reversed(copies):
        copy.wait()
    picks = []
    for route in (tuple(range(owners)),) + routes("tmpl", owners):
        target = lookup(route, me)
        local = jnp.full((ROWS, tall), -1, jnp.int32)
        for j in range(capacity):
            local = jnp.where(row == j, choice[0, 0, target, j], local)
        picks.append(jnp.where(local == column, 1.0, 0.0))
    picks = jnp.concatenate(picks, axis=0).astype(jnp.bfloat16)
    records = jnp.pad(taken[...].astype(jnp.float32), ((0, tall - high), (0, 0))).astype(jnp.bfloat16)
    picked = jnp.dot(picks, records, preferred_element_type=jnp.float32)
    for i, out in enumerate(outs):
        out[...] = picked[i * ROWS : (i + 1) * ROWS].astype(jnp.bfloat16)


def prepare(
    owners, capacity, tlen, templates, lists, moveouts, weights, bands, box, scale, totals, table, rows, taken, entries, shifts, factors, sems
):
    copies = fetch((templates, lists, moveouts, weights), (taken, entries, shifts, factors), sems)
    count, slots, _ = taken.shape
    pairs = count * slots
    depth = box.shape[0]
    groups = LAGS // STEP
    tap = lax.broadcasted_iota(jnp.int32, (depth, LANES), 0) - lax.broadcasted_iota(jnp.int32, (depth, LANES), 1) % STEP
    box[...] = jnp.where((tap >= 0) & (tap < tlen), 1.0, 0.0).astype(jnp.bfloat16)
    rows[...] = jnp.zeros_like(rows)
    for copy in copies:
        copy.wait()
    for m in range(count):
        rows[m * slots : (m + 1) * slots, :tlen] = taken[m].astype(jnp.float32)
    row = lax.broadcasted_iota(jnp.int32, (LANES, LANES), 0)
    lane = lax.broadcasted_iota(jnp.int32, (LANES, LANES), 1)
    late = row >= lane % STEP
    mirror = jnp.where(row + lane == LANES - 1, 1.0, 0.0).astype(jnp.bfloat16)
    zero = jnp.zeros((LANES, LANES), jnp.float32)
    values = rows[...]
    power = jnp.sum(values * values, axis=1, keepdims=True) / tlen
    factor = 1.0 / (jnp.sqrt(jnp.float32(tlen)) * jnp.sqrt(power + EPS))
    me = lax.axis_index("tmpl")
    turns = LANES // STEP
    sources = [me] + [lookup([route.index(i) for i in range(owners)], me) for route in routes("tmpl", owners)]
    for p in range(pairs):
        m, j = p // slots, p % slots
        source, slot = entries[j, m] // capacity, entries[j, m] % capacity
        for i in range(owners):
            slot = jnp.where(source == sources[i], slot % capacity + i * ROWS, slot)
        for h in range(turns):
            shift = shifts[j, m] + h * STEP
            q = p * turns + h
            table[q : q + 1, :] = jnp.full((1, LANES), slot + (shift // LANES) * owners * ROWS)
            table[turns * pairs + q : turns * pairs + q + 1, :] = jnp.full((1, LANES), (LANES - shift % LANES) % LANES)
        weight = factors[j, m].astype(jnp.float32)
        scale[p * groups : (p + 1) * groups, :] = jnp.broadcast_to(factor[p : p + 1] * weight, (groups, LANES))
    turned = [
        jnp.dot(values[:, d * LANES : (d + 1) * LANES].astype(jnp.bfloat16), mirror, preferred_element_type=jnp.float32)
        for d in range(-(-tlen // LANES))
    ]
    for c in range(pairs // turns):
        j, m = c // (count // turns), c % (count // turns) * turns
        before = zero
        for d in range(depth // LANES):
            now = zero
            if d * LANES < tlen:
                for h in range(turns):
                    back = turned[d][(m + h) * slots + j : (m + h) * slots + j + 1, :]
                    other = pltpu.roll(jnp.broadcast_to(back, (LANES, LANES)), 1 + h * STEP, axis=1, stride=1, stride_axis=0)
                    now = jnp.where(lane < h * STEP, now, other)
            bands[d * LANES : (d + 1) * LANES, c * LANES : (c + 1) * LANES] = jnp.where(late, now, before).astype(jnp.bfloat16)
            before = now
    for m in range(count):
        total = jnp.int32(0)
        for j in range(slots):
            total += factors[j, m] * factors[j, m]
        totals[m : m + 1, :] = jnp.full((1, LANES), total.astype(jnp.float32))


def correlate(owners, columns, tlen, count, slots, table, *refs):
    packed, refs = refs[:owners], refs[owners:]
    bands, box, scale, totals = refs[:4]
    outs, (lanes, taps, squares, stacks, sums, blocks) = refs[4:-6], refs[-6:]
    column = lax.axis_index("chan")
    pairs = count * slots
    depth = box.shape[0]
    pieces = packed[0].shape[1] // LANES
    stride = owners * ROWS
    groups = LAGS // STEP
    turns = LANES // STEP
    reach = LAGS // LANES + depth // LANES - 1
    for i in range(owners):
        wide = packed[i][...].astype(jnp.float32)
        for d in range(pieces):
            lanes[d * stride + i * ROWS : d * stride + (i + 1) * ROWS, :] = wide[:, d * LANES : (d + 1) * LANES]
    lanes[pieces * stride :, :] = jnp.zeros((stride, LANES), jnp.float32)
    places = table[...]
    lane = lax.broadcasted_iota(jnp.int32, (reach, LANES), 1)
    for p in range(pairs):
        for h in range(turns):
            first = places[p * turns + h, 0]
            back = places[turns * pairs + p * turns + h, 0]
            low = pltpu.roll(lanes[pl.ds(first, reach, stride=stride), :], back, axis=1)
            up = pltpu.roll(lanes[pl.ds(first + stride, reach, stride=stride), :], back, axis=1)
            stacks[p, pl.ds(h, reach, stride=turns), :] = jnp.where((lane < back) | (back == 0), low, up)
        for d in range(depth // LANES):
            piece = stacks[p, d * turns : d * turns + groups, :]
            taps[p * groups : (p + 1) * groups, d * LANES : (d + 1) * LANES] = piece
            squares[p * groups : (p + 1) * groups, d * LANES : (d + 1) * LANES] = piece * piece
    square = squares[...]
    main = square.astype(jnp.bfloat16)
    left = (square - main.astype(jnp.float32)).astype(jnp.bfloat16)
    energy = jnp.dot(jnp.concatenate([main, left], axis=0), box[...], preferred_element_type=jnp.float32)
    energy = energy[: pairs * groups] + energy[pairs * groups :]
    norm = scale[...] * lax.rsqrt(energy * (1.0 / tlen) + EPS)
    product = jnp.dot(taps[...].astype(jnp.bfloat16), bands[...], preferred_element_type=jnp.float32)
    front = lax.broadcasted_iota(jnp.int32, (LAGS // LANES, LANES), 1) < STEP
    for m in range(count):
        both = jnp.zeros((groups, LANES), jnp.float32)
        for j in range(slots):
            rows = slice((m * slots + j) * groups, (m * slots + j + 1) * groups)
            c = j * (count // turns) + m // turns
            both += product[rows, c * LANES : (c + 1) * LANES] * norm[rows, :]
        sums[m] = both
        even = sums[m, pl.ds(0, LAGS // LANES, stride=turns), :]
        odd = sums[m, pl.ds(1, LAGS // LANES, stride=turns), :]
        if m % turns:
            even = pltpu.roll(even, STEP, axis=1)
        else:
            odd = pltpu.roll(odd, STEP, axis=1)
        blocks[:, m, :] = jnp.where(front, even, odd)
        blocks[:, count + m, :] = jnp.broadcast_to(totals[m : m + 1, :], (LAGS // LANES, LANES))
    width = LAGS // columns
    share = LANES // width

    def block(target):
        part = blocks[target // share]
        chosen = part[:, :width]
        for s in range(1, share):
            chosen = jnp.where(target % share == s, part[:, s * width : (s + 1) * width], chosen)
        return chosen

    outs[-1][...] = block(column)
    if ("chan", columns) in ROUTES:
        for out, route in zip(outs, routes("chan", columns)):
            out[...] = block(lookup(route, column))
        return
    distance = 1
    for out in outs[:-1]:
        for q in range(out.shape[0]):
            out[q] = block(column ^ (distance * (2 * q + 1)))
        distance *= 2


def shards(waveforms, templates, selection, channel_list, moveouts, weights):
    owners = lax.axis_size("tmpl")
    columns = lax.axis_size("chan")
    count, slots, tlen = templates.shape
    pairs = count * slots
    groups = LAGS // STEP
    width = LAGS // columns
    samples = waveforms.shape[1]
    capacity = selection.shape[3]
    depth = -(-(tlen + STEP - 1) // LANES) * LANES
    pieces = samples // LANES

    def call(kernel, name, ins, outs, scratch, arguments, cost=None):
        if ins is HBM:
            arguments = [pltpu.with_memory_space_constraint(x, pltpu.HBM) for x in arguments]
        single = not isinstance(outs, tuple)
        return pl.pallas_call(
            kernel,
            out_shape=outs,
            in_specs=[ins] * len(arguments),
            out_specs=VMEM if single else (VMEM,) * len(outs),
            scratch_shapes=scratch,
            compiler_params=PARAMS,
            cost_estimate=cost,
            name=name,
        )(*arguments)

    rows = jax.ShapeDtypeStruct((ROWS, samples), waveforms.dtype)
    own, *outgoing = call(
        pack,
        "pack",
        HBM,
        (rows,) * owners,
        [
            pltpu.VMEM(waveforms.shape, waveforms.dtype),
            pltpu.SMEM(selection.shape, selection.dtype),
            pltpu.SemaphoreType.DMA((2,)),
        ],
        (waveforms, selection),
    )
    bands, box, scale, totals, table = call(
        functools.partial(prepare, owners, capacity, tlen),
        "prepare",
        HBM,
        (
            jax.ShapeDtypeStruct((depth, pairs * STEP), jnp.bfloat16),
            jax.ShapeDtypeStruct((depth, LANES), jnp.bfloat16),
            jax.ShapeDtypeStruct((pairs * groups, LANES), jnp.float32),
            jax.ShapeDtypeStruct((count, LANES), jnp.float32),
            jax.ShapeDtypeStruct((2 * pairs * (LANES // STEP), LANES), jnp.int32),
        ),
        [
            pltpu.VMEM((pairs, depth), jnp.float32),
            pltpu.VMEM(templates.shape, templates.dtype),
            pltpu.SMEM((slots, count), jnp.int32),
            pltpu.SMEM((slots, count), jnp.int32),
            pltpu.SMEM((slots, count), jnp.int32),
            pltpu.SemaphoreType.DMA((4,)),
        ],
        (templates, channel_list.T, moveouts.T, weights.T),
        pl.CostEstimate(flops=2_000_000, bytes_accessed=2_000_000, transcendentals=0),
    )
    packed = [own] + [send(x, "tmpl", route) for x, route in zip(outgoing, routes("tmpl", owners))]
    sizes = []
    while (columns >> len(sizes)) > 1:
        sizes.append(columns >> (len(sizes) + 1))
    shapes = [(s, 2 * count, width) for s in sizes] + [(2 * count, width)]
    if ("chan", columns) in ROUTES:
        shapes = [(2 * count, width)] * columns
    parts = call(
        functools.partial(correlate, owners, columns, tlen, count, slots),
        "correlate",
        VMEM,
        tuple(jax.ShapeDtypeStruct(s, jnp.float32) for s in shapes),
        [
            pltpu.VMEM(((pieces + 1) * owners * ROWS, LANES), jnp.float32),
            pltpu.VMEM((pairs * groups, depth), jnp.float32),
            pltpu.VMEM((pairs * groups, depth), jnp.float32),
            pltpu.VMEM((pairs, 32, LANES), jnp.float32),
            pltpu.VMEM((count, groups, LANES), jnp.float32),
            pltpu.VMEM((LAGS // LANES, 2 * count, LANES), jnp.float32),
        ],
        (table, *packed, bands, box, scale, totals),
    )
    stages, own = list(parts[:-1]), [parts[-1]]
    if ("chan", columns) in ROUTES:
        for part, route in zip(stages, routes("chan", columns)):
            own.append(send(part, "chan", route))
        stages = []
    for i in range(len(stages)):
        arrived = exchange(stages[i], "chan", 1 << i)
        own.append(arrived[0])
        for later in range(i + 1, len(stages)):
            step = 1 << (later - i)
            stages[later] = stages[later] + arrived[step // 2 :: step]
    top = sum(x[:count] for x in own)
    return top / jnp.sqrt(sum(x[count:] for x in own))


def solution(mesh):
    placed = (
        P(("parts", "tmpl", "chan"), None),
        P(("parts", "tmpl"), "chan", None),
        P(("parts", "tmpl"), "chan", None, None),
        P(("parts", "tmpl"), "chan"),
        P(("parts", "tmpl"), "chan"),
        P(("parts", "tmpl"), "chan"),
    )
    return jax.shard_map(
        shards, mesh=mesh, in_specs=placed, out_specs=P(("parts", "tmpl"), "chan"), check_vma=False
    )
```

```python
import functools

import jax
import jax.numpy as jnp
from jax import lax
from jax.experimental import pallas as pl
from jax.experimental.pallas import tpu as pltpu
from jax.sharding import PartitionSpec as P

LAGS = 512
EPS = 1e-06
LANES = 128
PARAMS = pltpu.CompilerParams(vmem_limit_bytes=8 * 1024 * 1024)
STEP = 64
ROUTES = {
    ("tmpl", 4): ((3, 2, 0, 1), (2, 3, 1, 0), (1, 0, 3, 2)),
    ("chan", 4): ((2, 3, 1, 0), (3, 2, 0, 1), (1, 0, 3, 2)),
}
ROWS = 8
VMEM = pl.BlockSpec(memory_space=pltpu.VMEM)
HBM = pl.BlockSpec(memory_space=pltpu.HBM)


def exchange(value, axis, distance):
    size = lax.axis_size(axis)
    return lax.ppermute(value, axis, [(i, i ^ distance) for i in range(size)])


def routes(axis, size):
    return ROUTES.get((axis, size), tuple(tuple(i ^ k for i in range(size)) for k in range(1, size)))


def send(value, axis, route):
    return lax.ppermute(value, axis, list(enumerate(route)))


def lookup(values, place):
    found = jnp.int32(values[0])
    for i in range(1, len(values)):
        found = jnp.where(place == i, values[i], found)
    return found


def fetch(sources, targets, sems):
    copies = [pltpu.make_async_copy(a, b, sems.at[i]) for i, (a, b) in enumerate(zip(sources, targets))]
    for copy in copies:
        copy.start()
    return copies


def pack(waveforms, selection, *refs):
    outs, (taken, choice, sems) = refs[:-3], refs[-3:]
    copies = fetch((waveforms, selection), (taken, choice), sems)
    high, samples = waveforms.shape
    _, _, owners, capacity = choice.shape
    me = lax.axis_index("tmpl")
    tall = -(-high // 16) * 16
    row = lax.broadcasted_iota(jnp.int32, (ROWS, tall), 0)
    column = lax.broadcasted_iota(jnp.int32, (ROWS, tall), 1)
    copies[1].wait()
    picks = []
    for route in (tuple(range(owners)),) + routes("tmpl", owners):
        target = lookup(route, me)
        local = jnp.full((ROWS, tall), -1, jnp.int32)
        for j in range(capacity):
            local = jnp.where(row == j, choice[0, 0, target, j], local)
        picks.append(jnp.where(local == column, 1.0, 0.0))
    picks = jnp.concatenate(picks, axis=0).astype(jnp.bfloat16)
    copies[0].wait()
    records = jnp.pad(taken[...].astype(jnp.float32), ((0, tall - high), (0, 0))).astype(jnp.bfloat16)
    picked = jnp.dot(picks, records, preferred_element_type=jnp.float32)
    for i, out in enumerate(outs):
        out[...] = picked[i * ROWS : (i + 1) * ROWS].astype(jnp.bfloat16)


def prepare(
    owners, capacity, tlen, templates, lists, moveouts, weights, bands, box, scale, totals, table, rows, taken, entries, shifts, factors, sems
):
    copies = fetch((templates, lists, moveouts, weights), (taken, entries, shifts, factors), sems)
    count, slots, _ = taken.shape
    pairs = count * slots
    depth = box.shape[0]
    groups = LAGS // STEP
    tap = lax.broadcasted_iota(jnp.int32, (depth, LANES), 0) - lax.broadcasted_iota(jnp.int32, (depth, LANES), 1) % STEP
    box[...] = jnp.where((tap >= 0) & (tap < tlen), 1.0, 0.0).astype(jnp.bfloat16)
    rows[...] = jnp.zeros_like(rows)
    for copy in copies:
        copy.wait()
    for m in range(count):
        rows[m * slots : (m + 1) * slots, :tlen] = taken[m].astype(jnp.float32)
    row = lax.broadcasted_iota(jnp.int32, (LANES, LANES), 0)
    lane = lax.broadcasted_iota(jnp.int32, (LANES, LANES), 1)
    late = row >= lane % STEP
    mirror = jnp.where(row + lane == LANES - 1, 1.0, 0.0).astype(jnp.bfloat16)
    zero = jnp.zeros((LANES, LANES), jnp.float32)
    values = rows[...]
    power = jnp.sum(values * values, axis=1, keepdims=True) / tlen
    factor = 1.0 / (jnp.sqrt(jnp.float32(tlen)) * jnp.sqrt(power + EPS))
    me = lax.axis_index("tmpl")
    turns = LANES // STEP
    sources = [me] + [lookup([route.index(i) for i in range(owners)], me) for route in routes("tmpl", owners)]
    for p in range(pairs):
        m, j = p // slots, p % slots
        source, slot = entries[j, m] // capacity, entries[j, m] % capacity
        for i in range(owners):
            slot = jnp.where(source == sources[i], slot % capacity + i * ROWS, slot)
        for h in range(turns):
            shift = shifts[j, m] + h * STEP
            q = p * turns + h
            table[q : q + 1, :] = jnp.full((1, LANES), slot + (shift // LANES) * owners * ROWS)
            table[turns * pairs + q : turns * pairs + q + 1, :] = jnp.full((1, LANES), (LANES - shift % LANES) % LANES)
        weight = factors[j, m].astype(jnp.float32)
        scale[p * groups : (p + 1) * groups, :] = jnp.broadcast_to(factor[p : p + 1] * weight, (groups, LANES))
    turned = [
        jnp.dot(values[:, d * LANES : (d + 1) * LANES].astype(jnp.bfloat16), mirror, preferred_element_type=jnp.float32)
        for d in range(-(-tlen // LANES))
    ]
    for c in range(pairs // turns):
        j, m = c // (count // turns), c % (count // turns) * turns
        before = zero
        for d in range(depth // LANES):
            now = zero
            if d * LANES < tlen:
                for h in range(turns):
                    back = turned[d][(m + h) * slots + j : (m + h) * slots + j + 1, :]
                    other = pltpu.roll(jnp.broadcast_to(back, (LANES, LANES)), 1 + h * STEP, axis=1, stride=1, stride_axis=0)
                    now = jnp.where(lane < h * STEP, now, other)
            bands[d * LANES : (d + 1) * LANES, c * LANES : (c + 1) * LANES] = jnp.where(late, now, before).astype(jnp.bfloat16)
            before = now
    for m in range(count):
        total = jnp.int32(0)
        for j in range(slots):
            total += factors[j, m] * factors[j, m]
        totals[m : m + 1, :] = jnp.full((1, LANES), total.astype(jnp.float32))


def correlate(owners, columns, tlen, count, slots, table, *refs):
    packed, refs = refs[:owners], refs[owners:]
    bands, box, scale, totals = refs[:4]
    outs, (lanes, stacks, sums, blocks) = refs[4:-4], refs[-4:]
    column = lax.axis_index("chan")
    pairs = count * slots
    depth = box.shape[0]
    pieces = packed[0].shape[1] // LANES
    stride = owners * ROWS
    groups = LAGS // STEP
    turns = LANES // STEP
    reach = LAGS // LANES + depth // LANES - 1
    for i in range(owners):
        wide = packed[i][...].astype(jnp.float32)
        for d in range(pieces):
            lanes[d * stride + i * ROWS : d * stride + (i + 1) * ROWS, :] = wide[:, d * LANES : (d + 1) * LANES]
    lanes[pieces * stride : (pieces + 1) * stride, :] = jnp.zeros((stride, LANES), jnp.float32)
    places = table[...]
    lane = lax.broadcasted_iota(jnp.int32, (reach, LANES), 1)
    for p in range(pairs):
        for h in range(turns):
            first = places[p * turns + h, 0]
            back = places[turns * pairs + p * turns + h, 0]
            low = pltpu.roll(lanes[pl.ds(first, reach, stride=stride), :], back, axis=1)
            up = pltpu.roll(lanes[pl.ds(first + stride, reach, stride=stride), :], back, axis=1)
            stacks[p, pl.ds(h, reach, stride=turns), :] = jnp.where((lane < back) | (back == 0), low, up)
    taps = [
        jnp.concatenate([stacks[p, d * turns : d * turns + groups, :] for d in range(depth // LANES)], axis=1) for p in range(pairs)
    ]
    taps = jnp.concatenate(taps, axis=0)
    square = taps * taps
    main = square.astype(jnp.bfloat16)
    left = (square - main.astype(jnp.float32)).astype(jnp.bfloat16)
    energy = jnp.dot(jnp.concatenate([main, left], axis=0), box[...], preferred_element_type=jnp.float32)
    energy = energy[: pairs * groups] + energy[pairs * groups :]
    norm = scale[...] * lax.rsqrt(energy * (1.0 / tlen) + EPS)
    product = jnp.dot(taps.astype(jnp.bfloat16), bands[...], preferred_element_type=jnp.float32)
    front = lax.broadcasted_iota(jnp.int32, (LAGS // LANES, LANES), 1) < STEP
    for m in range(count):
        both = jnp.zeros((groups, LANES), jnp.float32)
        for j in range(slots):
            rows = slice((m * slots + j) * groups, (m * slots + j + 1) * groups)
            c = j * (count // turns) + m // turns
            both += product[rows, c * LANES : (c + 1) * LANES] * norm[rows, :]
        sums[m, :groups, :] = both
        even = sums[m, pl.ds(0, LAGS // LANES, stride=turns), :]
        odd = sums[m, pl.ds(1, LAGS // LANES, stride=turns), :]
        if m % turns:
            even = pltpu.roll(even, STEP, axis=1)
        else:
            odd = pltpu.roll(odd, STEP, axis=1)
        blocks[: LAGS // LANES, m, :] = jnp.where(front, even, odd)
        blocks[: LAGS // LANES, count + m, :] = jnp.broadcast_to(totals[m : m + 1, :], (LAGS // LANES, LANES))
    width = LAGS // columns
    share = LANES // width

    def block(target):
        part = blocks[target // share]
        chosen = part[:, :width]
        for s in range(1, share):
            chosen = jnp.where(target % share == s, part[:, s * width : (s + 1) * width], chosen)
        return chosen

    outs[-1][...] = block(column)
    if ("chan", columns) in ROUTES:
        for out, route in zip(outs, routes("chan", columns)):
            out[...] = block(lookup(route, column))
        return
    distance = 1
    for out in outs[:-1]:
        for q in range(out.shape[0]):
            out[q] = block(column ^ (distance * (2 * q + 1)))
        distance *= 2


def shards(waveforms, templates, selection, channel_list, moveouts, weights):
    owners = lax.axis_size("tmpl")
    columns = lax.axis_size("chan")
    count, slots, tlen = templates.shape
    pairs = count * slots
    groups = LAGS // STEP
    width = LAGS // columns
    samples = waveforms.shape[1]
    capacity = selection.shape[3]
    depth = -(-(tlen + STEP - 1) // LANES) * LANES
    pieces = samples // LANES

    def call(kernel, name, ins, outs, scratch, arguments, cost=None):
        if ins is HBM:
            arguments = [pltpu.with_memory_space_constraint(x, pltpu.HBM) for x in arguments]
        single = not isinstance(outs, tuple)
        return pl.pallas_call(
            kernel,
            out_shape=outs,
            in_specs=[ins] * len(arguments),
            out_specs=VMEM if single else (VMEM,) * len(outs),
            scratch_shapes=scratch,
            compiler_params=PARAMS,
            cost_estimate=cost,
            name=name,
        )(*arguments)

    rows = jax.ShapeDtypeStruct((ROWS, samples), waveforms.dtype)
    own, *outgoing = call(
        pack,
        "pack",
        HBM,
        (rows,) * owners,
        [
            pltpu.VMEM(waveforms.shape, waveforms.dtype),
            pltpu.SMEM(selection.shape, selection.dtype),
            pltpu.SemaphoreType.DMA((2,)),
        ],
        (waveforms, selection),
    )
    bands, box, scale, totals, table = call(
        functools.partial(prepare, owners, capacity, tlen),
        "prepare",
        HBM,
        (
            jax.ShapeDtypeStruct((depth, pairs * STEP), jnp.bfloat16),
            jax.ShapeDtypeStruct((depth, LANES), jnp.bfloat16),
            jax.ShapeDtypeStruct((pairs * groups, LANES), jnp.float32),
            jax.ShapeDtypeStruct((count, LANES), jnp.float32),
            jax.ShapeDtypeStruct((2 * pairs * (LANES // STEP), LANES), jnp.int32),
        ),
        [
            pltpu.VMEM((pairs, depth), jnp.float32),
            pltpu.VMEM(templates.shape, templates.dtype),
            pltpu.SMEM((slots, count), jnp.int32),
            pltpu.SMEM((slots, count), jnp.int32),
            pltpu.SMEM((slots, count), jnp.int32),
            pltpu.SemaphoreType.DMA((4,)),
        ],
        (templates, channel_list.T, moveouts.T, weights.T),
        pl.CostEstimate(flops=2_000_000, bytes_accessed=2_000_000, transcendentals=0),
    )
    packed = [own] + [send(x, "tmpl", route) for x, route in zip(outgoing, routes("tmpl", owners))]
    sizes = []
    while (columns >> len(sizes)) > 1:
        sizes.append(columns >> (len(sizes) + 1))
    shapes = [(s, 2 * count, width) for s in sizes] + [(2 * count, width)]
    if ("chan", columns) in ROUTES:
        shapes = [(2 * count, width)] * columns
    parts = call(
        functools.partial(correlate, owners, columns, tlen, count, slots),
        "correlate",
        VMEM,
        tuple(jax.ShapeDtypeStruct(s, jnp.float32) for s in shapes),
        [
            pltpu.VMEM(((pieces + 8) * owners * ROWS, LANES), jnp.float32),
            pltpu.VMEM((pairs, 32, LANES), jnp.float32),
            pltpu.VMEM((count, 2 * groups, LANES), jnp.float32),
            pltpu.VMEM((2 * LAGS // LANES, 2 * count, LANES), jnp.float32),
        ],
        (table, *packed, bands, box, scale, totals),
    )
    stages, own = list(parts[:-1]), [parts[-1]]
    if ("chan", columns) in ROUTES:
        for part, route in zip(stages, routes("chan", columns)):
            own.append(send(part, "chan", route))
        stages = []
    for i in range(len(stages)):
        arrived = exchange(stages[i], "chan", 1 << i)
        own.append(arrived[0])
        for later in range(i + 1, len(stages)):
            step = 1 << (later - i)
            stages[later] = stages[later] + arrived[step // 2 :: step]
    top = sum(x[:count] for x in own)
    return top / jnp.sqrt(sum(x[count:] for x in own))


def solution(mesh):
    placed = (
        P(("parts", "tmpl", "chan"), None),
        P(("parts", "tmpl"), "chan", None),
        P(("parts", "tmpl"), "chan", None, None),
        P(("parts", "tmpl"), "chan"),
        P(("parts", "tmpl"), "chan"),
        P(("parts", "tmpl"), "chan"),
    )
    return jax.shard_map(
        shards, mesh=mesh, in_specs=placed, out_specs=P(("parts", "tmpl"), "chan"), check_vma=False
    )
```

```python
import functools

import jax
import jax.numpy as jnp
from jax import lax
from jax.experimental import pallas as pl
from jax.experimental.pallas import tpu as pltpu
from jax.sharding import PartitionSpec as P

LAGS = 512
EPS = 1e-06
LANES = 128
PARAMS = pltpu.CompilerParams(vmem_limit_bytes=8 * 1024 * 1024)
STEP = 64
ROUTES = {
    ("tmpl", 4): ((3, 2, 0, 1), (2, 3, 1, 0), (1, 0, 3, 2)),
    ("chan", 4): ((2, 3, 1, 0), (3, 2, 0, 1), (1, 0, 3, 2)),
}
ROWS = 8
VMEM = pl.BlockSpec(memory_space=pltpu.VMEM)
HBM = pl.BlockSpec(memory_space=pltpu.HBM)


def exchange(value, axis, distance):
    size = lax.axis_size(axis)
    return lax.ppermute(value, axis, [(i, i ^ distance) for i in range(size)])


def routes(axis, size):
    return ROUTES.get((axis, size), tuple(tuple(i ^ k for i in range(size)) for k in range(1, size)))


def send(value, axis, route):
    return lax.ppermute(value, axis, list(enumerate(route)))


def lookup(values, place):
    found = jnp.int32(values[0])
    for i in range(1, len(values)):
        found = jnp.where(place == i, values[i], found)
    return found


def fetch(sources, targets, sems):
    copies = [pltpu.make_async_copy(a, b, sems.at[i]) for i, (a, b) in enumerate(zip(sources, targets))]
    for copy in copies:
        copy.start()
    return copies


def pack(waveforms, selection, *refs):
    outs, (taken, choice, sems) = refs[:-3], refs[-3:]
    copies = fetch((waveforms, selection), (taken, choice), sems)
    high, samples = waveforms.shape
    _, _, owners, capacity = choice.shape
    me = lax.axis_index("tmpl")
    tall = -(-high // 16) * 16
    row = lax.broadcasted_iota(jnp.int32, (ROWS, tall), 0)
    column = lax.broadcasted_iota(jnp.int32, (ROWS, tall), 1)
    copies[1].wait()
    picks = []
    for route in (tuple(range(owners)),) + routes("tmpl", owners):
        target = lookup(route, me)
        local = jnp.full((ROWS, tall), -1, jnp.int32)
        for j in range(capacity):
            local = jnp.where(row == j, choice[0, 0, target, j], local)
        picks.append(jnp.where(local == column, 1.0, 0.0))
    picks = jnp.concatenate(picks, axis=0).astype(jnp.bfloat16)
    copies[0].wait()
    records = jnp.pad(taken[...].astype(jnp.float32), ((0, tall - high), (0, 0))).astype(jnp.bfloat16)
    picked = jnp.dot(picks, records, preferred_element_type=jnp.float32)
    for i, out in enumerate(outs):
        out[...] = picked[i * ROWS : (i + 1) * ROWS].astype(jnp.bfloat16)


def prepare(
    owners, capacity, tlen, templates, lists, moveouts, weights, bands, box, scale, totals, table, rows, taken, entries, shifts, factors, sems
):
    copies = fetch((templates, lists, moveouts, weights), (taken, entries, shifts, factors), sems)
    count, slots, _ = taken.shape
    pairs = count * slots
    depth = box.shape[0]
    groups = LAGS // STEP
    tap = lax.broadcasted_iota(jnp.int32, (depth, LANES), 0) - lax.broadcasted_iota(jnp.int32, (depth, LANES), 1) % STEP
    box[...] = jnp.where((tap >= 0) & (tap < tlen), 1.0, 0.0).astype(jnp.bfloat16)
    rows[...] = jnp.zeros_like(rows)
    for copy in copies:
        copy.wait()
    for m in range(count):
        rows[m * slots : (m + 1) * slots, :tlen] = taken[m].astype(jnp.float32)
    row = lax.broadcasted_iota(jnp.int32, (LANES, LANES), 0)
    lane = lax.broadcasted_iota(jnp.int32, (LANES, LANES), 1)
    late = row >= lane % STEP
    mirror = jnp.where(row + lane == LANES - 1, 1.0, 0.0).astype(jnp.bfloat16)
    zero = jnp.zeros((LANES, LANES), jnp.float32)
    values = rows[...]
    power = jnp.sum(values * values, axis=1, keepdims=True) / tlen
    factor = 1.0 / (jnp.sqrt(jnp.float32(tlen)) * jnp.sqrt(power + EPS))
    me = lax.axis_index("tmpl")
    turns = LANES // STEP
    sources = [me] + [lookup([route.index(i) for i in range(owners)], me) for route in routes("tmpl", owners)]
    for p in range(pairs):
        m, j = p // slots, p % slots
        source, slot = entries[j, m] // capacity, entries[j, m] % capacity
        for i in range(owners):
            slot = jnp.where(source == sources[i], slot % capacity + i * ROWS, slot)
        shift = shifts[j, m]
        row_of = slot + (shift // LANES) * owners * ROWS
        table[p : p + 1, :] = jnp.full((1, LANES), row_of * LANES + (LANES - shift % LANES) % LANES)
        weight = factors[j, m].astype(jnp.float32)
        scale[p * groups : (p + 1) * groups, :] = jnp.broadcast_to(factor[p : p + 1] * weight, (groups, LANES))
    turned = [
        jnp.dot(values[:, d * LANES : (d + 1) * LANES].astype(jnp.bfloat16), mirror, preferred_element_type=jnp.float32)
        for d in range(-(-tlen // LANES))
    ]
    for c in range(pairs // turns):
        j, m = c // (count // turns), c % (count // turns) * turns
        before = zero
        for d in range(depth // LANES):
            now = zero
            if d * LANES < tlen:
                for h in range(turns):
                    back = turned[d][(m + h) * slots + j : (m + h) * slots + j + 1, :]
                    other = pltpu.roll(jnp.broadcast_to(back, (LANES, LANES)), 1 + h * STEP, axis=1, stride=1, stride_axis=0)
                    now = jnp.where(lane < h * STEP, now, other)
            bands[d * LANES : (d + 1) * LANES, c * LANES : (c + 1) * LANES] = jnp.where(late, now, before).astype(jnp.bfloat16)
            before = now
    for m in range(count):
        total = jnp.int32(0)
        for j in range(slots):
            total += factors[j, m] * factors[j, m]
        totals[m : m + 1, :] = jnp.full((1, LANES), total.astype(jnp.float32))


def correlate(owners, columns, tlen, count, slots, table, *refs):
    packed, refs = refs[:owners], refs[owners:]
    bands, box, scale, totals = refs[:4]
    outs, (lanes, stacks, sums, blocks) = refs[4:-4], refs[-4:]
    column = lax.axis_index("chan")
    pairs = count * slots
    depth = box.shape[0]
    pieces = packed[0].shape[1] // LANES
    stride = owners * ROWS
    groups = LAGS // STEP
    turns = LANES // STEP
    reach = LAGS // LANES + depth // LANES - 1
    for i in range(owners):
        wide = packed[i][...].astype(jnp.float32)
        for d in range(pieces):
            lanes[d * stride + i * ROWS : d * stride + (i + 1) * ROWS, :] = wide[:, d * LANES : (d + 1) * LANES]
    lanes[pieces * stride : (pieces + 1) * stride, :] = jnp.zeros((stride, LANES), jnp.float32)
    places = table[...]
    lane = lax.broadcasted_iota(jnp.int32, (reach, LANES), 1)
    for p in range(pairs):
        place = places[p, 0]
        first, back = lax.shift_right_logical(place, 7), lax.bitwise_and(place, LANES - 1)
        for h in range(turns):
            if h:
                first = jnp.where((back > 0) & (back <= STEP), first + stride, first)
                back = lax.bitwise_xor(back, STEP)
            low = lanes[pl.ds(first, reach, stride=stride), :]
            up = lanes[pl.ds(first + stride, reach, stride=stride), :]
            rest = lax.bitwise_and(LANES - back, LANES - 1)
            stacks[p, pl.ds(h, reach, stride=turns), :] = pltpu.roll(jnp.where(lane >= rest, low, up), back, axis=1)
    taps = [
        jnp.concatenate([stacks[p, d * turns : d * turns + groups, :] for d in range(depth // LANES)], axis=1) for p in range(pairs)
    ]
    taps = jnp.concatenate(taps, axis=0)
    square = taps * taps
    main = square.astype(jnp.bfloat16)
    left = (square - main.astype(jnp.float32)).astype(jnp.bfloat16)
    energy = jnp.dot(jnp.concatenate([main, left], axis=0), box[...], preferred_element_type=jnp.float32)
    energy = energy[: pairs * groups] + energy[pairs * groups :]
    norm = scale[...] * lax.rsqrt(energy * (1.0 / tlen) + EPS)
    product = jnp.dot(taps.astype(jnp.bfloat16), bands[...], preferred_element_type=jnp.float32)
    front = lax.broadcasted_iota(jnp.int32, (LAGS // LANES, LANES), 1) < STEP
    for m in range(count):
        both = jnp.zeros((groups, LANES), jnp.float32)
        for j in range(slots):
            rows = slice((m * slots + j) * groups, (m * slots + j + 1) * groups)
            c = j * (count // turns) + m // turns
            both += product[rows, c * LANES : (c + 1) * LANES] * norm[rows, :]
        sums[m, :groups, :] = both
        even = sums[m, pl.ds(0, LAGS // LANES, stride=turns), :]
        odd = sums[m, pl.ds(1, LAGS // LANES, stride=turns), :]
        if m % turns:
            even = pltpu.roll(even, STEP, axis=1)
        else:
            odd = pltpu.roll(odd, STEP, axis=1)
        blocks[: LAGS // LANES, m, :] = jnp.where(front, even, odd)
        blocks[: LAGS // LANES, count + m, :] = jnp.broadcast_to(totals[m : m + 1, :], (LAGS // LANES, LANES))
    width = LAGS // columns
    share = LANES // width

    def block(target):
        part = blocks[target // share]
        chosen = part[:, :width]
        for s in range(1, share):
            chosen = jnp.where(target % share == s, part[:, s * width : (s + 1) * width], chosen)
        return chosen

    outs[-1][...] = block(column)
    if ("chan", columns) in ROUTES:
        for out, route in zip(outs, routes("chan", columns)):
            out[...] = block(lookup(route, column))
        return
    distance = 1
    for out in outs[:-1]:
        for q in range(out.shape[0]):
            out[q] = block(column ^ (distance * (2 * q + 1)))
        distance *= 2


def shards(waveforms, templates, selection, channel_list, moveouts, weights):
    owners = lax.axis_size("tmpl")
    columns = lax.axis_size("chan")
    count, slots, tlen = templates.shape
    pairs = count * slots
    groups = LAGS // STEP
    width = LAGS // columns
    samples = waveforms.shape[1]
    capacity = selection.shape[3]
    depth = -(-(tlen + STEP - 1) // LANES) * LANES
    pieces = samples // LANES

    def call(kernel, name, ins, outs, scratch, arguments, cost=None):
        if ins is HBM:
            arguments = [pltpu.with_memory_space_constraint(x, pltpu.HBM) for x in arguments]
        single = not isinstance(outs, tuple)
        return pl.pallas_call(
            kernel,
            out_shape=outs,
            in_specs=[ins] * len(arguments),
            out_specs=VMEM if single else (VMEM,) * len(outs),
            scratch_shapes=scratch,
            compiler_params=PARAMS,
            cost_estimate=cost,
            name=name,
        )(*arguments)

    rows = jax.ShapeDtypeStruct((ROWS, samples), waveforms.dtype)
    own, *outgoing = call(
        pack,
        "pack",
        HBM,
        (rows,) * owners,
        [
            pltpu.VMEM(waveforms.shape, waveforms.dtype),
            pltpu.SMEM(selection.shape, selection.dtype),
            pltpu.SemaphoreType.DMA((2,)),
        ],
        (waveforms, selection),
    )
    bands, box, scale, totals, table = call(
        functools.partial(prepare, owners, capacity, tlen),
        "prepare",
        HBM,
        (
            jax.ShapeDtypeStruct((depth, pairs * STEP), jnp.bfloat16),
            jax.ShapeDtypeStruct((depth, LANES), jnp.bfloat16),
            jax.ShapeDtypeStruct((pairs * groups, LANES), jnp.float32),
            jax.ShapeDtypeStruct((count, LANES), jnp.float32),
            jax.ShapeDtypeStruct((pairs, LANES), jnp.int32),
        ),
        [
            pltpu.VMEM((pairs, depth), jnp.float32),
            pltpu.VMEM(templates.shape, templates.dtype),
            pltpu.SMEM((slots, count), jnp.int32),
            pltpu.SMEM((slots, count), jnp.int32),
            pltpu.SMEM((slots, count), jnp.int32),
            pltpu.SemaphoreType.DMA((4,)),
        ],
        (templates, channel_list.T, moveouts.T, weights.T),
        pl.CostEstimate(flops=2_000_000, bytes_accessed=2_000_000, transcendentals=0),
    )
    packed = [own] + [send(x, "tmpl", route) for x, route in zip(outgoing, routes("tmpl", owners))]
    sizes = []
    while (columns >> len(sizes)) > 1:
        sizes.append(columns >> (len(sizes) + 1))
    shapes = [(s, 2 * count, width) for s in sizes] + [(2 * count, width)]
    if ("chan", columns) in ROUTES:
        shapes = [(2 * count, width)] * columns
    parts = call(
        functools.partial(correlate, owners, columns, tlen, count, slots),
        "correlate",
        VMEM,
        tuple(jax.ShapeDtypeStruct(s, jnp.float32) for s in shapes),
        [
            pltpu.VMEM(((pieces + 8) * owners * ROWS, LANES), jnp.float32),
            pltpu.VMEM((pairs, 32, LANES), jnp.float32),
            pltpu.VMEM((count, 2 * groups, LANES), jnp.float32),
            pltpu.VMEM((2 * LAGS // LANES, 2 * count, LANES), jnp.float32),
        ],
        (table, *packed, bands, box, scale, totals),
    )
    stages, own = list(parts[:-1]), [parts[-1]]
    if ("chan", columns) in ROUTES:
        for part, route in zip(stages, routes("chan", columns)):
            own.append(send(part, "chan", route))
        stages = []
    for i in range(len(stages)):
        arrived = exchange(stages[i], "chan", 1 << i)
        own.append(arrived[0])
        for later in range(i + 1, len(stages)):
            step = 1 << (later - i)
            stages[later] = stages[later] + arrived[step // 2 :: step]
    top = sum(x[:count] for x in own)
    return top / jnp.sqrt(sum(x[count:] for x in own))


def solution(mesh):
    placed = (
        P(("parts", "tmpl", "chan"), None),
        P(("parts", "tmpl"), "chan", None),
        P(("parts", "tmpl"), "chan", None, None),
        P(("parts", "tmpl"), "chan"),
        P(("parts", "tmpl"), "chan"),
        P(("parts", "tmpl"), "chan"),
    )
    return jax.shard_map(
        shards, mesh=mesh, in_specs=placed, out_specs=P(("parts", "tmpl"), "chan"), check_vma=False
    )
```

```python
import functools

import jax
import jax.numpy as jnp
from jax import lax
from jax.experimental import pallas as pl
from jax.experimental.pallas import tpu as pltpu
from jax.sharding import PartitionSpec as P

LAGS = 512
EPS = 1e-06
LANES = 128
PARAMS = pltpu.CompilerParams(vmem_limit_bytes=8 * 1024 * 1024)
STEP = 64
ROUTES = {
    ("tmpl", 4): ((3, 2, 0, 1), (2, 3, 1, 0), (1, 0, 3, 2)),
    ("chan", 4): ((2, 3, 1, 0), (3, 2, 0, 1), (1, 0, 3, 2)),
}
ROWS = 8
VMEM = pl.BlockSpec(memory_space=pltpu.VMEM)
HBM = pl.BlockSpec(memory_space=pltpu.HBM)


def exchange(value, axis, distance):
    size = lax.axis_size(axis)
    return lax.ppermute(value, axis, [(i, i ^ distance) for i in range(size)])


def routes(axis, size):
    return ROUTES.get((axis, size), tuple(tuple(i ^ k for i in range(size)) for k in range(1, size)))


def send(value, axis, route):
    return lax.ppermute(value, axis, list(enumerate(route)))


def lookup(values, place):
    found = jnp.int32(values[0])
    for i in range(1, len(values)):
        found = jnp.where(place == i, values[i], found)
    return found


def fetch(sources, targets, sems):
    copies = [pltpu.make_async_copy(a, b, sems.at[i]) for i, (a, b) in enumerate(zip(sources, targets))]
    for copy in copies:
        copy.start()
    return copies


def pack(waveforms, selection, *refs):
    outs, (taken, choice, sems) = refs[:-3], refs[-3:]
    copies = fetch((waveforms, selection), (taken, choice), sems)
    high, samples = waveforms.shape
    _, _, owners, capacity = choice.shape
    me = lax.axis_index("tmpl")
    tall = -(-high // 16) * 16
    row = lax.broadcasted_iota(jnp.int32, (ROWS, tall), 0)
    column = lax.broadcasted_iota(jnp.int32, (ROWS, tall), 1)
    copies[1].wait()
    picks = []
    for route in (tuple(range(owners)),) + routes("tmpl", owners):
        target = lookup(route, me)
        local = jnp.full((ROWS, tall), -1, jnp.int32)
        for j in range(capacity):
            local = jnp.where(row == j, choice[0, 0, target, j], local)
        picks.append(jnp.where(local == column, 1.0, 0.0))
    picks = jnp.concatenate(picks, axis=0).astype(jnp.bfloat16)
    copies[0].wait()
    records = jnp.pad(taken[...].astype(jnp.float32), ((0, tall - high), (0, 0))).astype(jnp.bfloat16)
    picked = jnp.dot(picks, records, preferred_element_type=jnp.float32)
    for i, out in enumerate(outs):
        out[...] = picked[i * ROWS : (i + 1) * ROWS].astype(jnp.bfloat16)


def prepare(
    owners, capacity, tlen, templates, lists, moveouts, weights, bands, box, scale, totals, table, rows, taken, entries, shifts, factors, sems
):
    copies = fetch((templates, lists, moveouts, weights), (taken, entries, shifts, factors), sems)
    count, slots, _ = taken.shape
    pairs = count * slots
    depth = box.shape[0]
    groups = LAGS // STEP
    tap = lax.broadcasted_iota(jnp.int32, (depth, LANES), 0) - lax.broadcasted_iota(jnp.int32, (depth, LANES), 1) % STEP
    box[...] = jnp.where((tap >= 0) & (tap < tlen), 1.0, 0.0).astype(jnp.bfloat16)
    rows[...] = jnp.zeros_like(rows)
    for copy in copies:
        copy.wait()
    for m in range(count):
        rows[m * slots : (m + 1) * slots, :tlen] = taken[m].astype(jnp.float32)
    row = lax.broadcasted_iota(jnp.int32, (LANES, LANES), 0)
    lane = lax.broadcasted_iota(jnp.int32, (LANES, LANES), 1)
    late = row >= lane % STEP
    mirror = jnp.where(row + lane == LANES - 1, 1.0, 0.0).astype(jnp.bfloat16)
    zero = jnp.zeros((LANES, LANES), jnp.float32)
    values = rows[...]
    power = jnp.sum(values * values, axis=1, keepdims=True) / tlen
    factor = 1.0 / (jnp.sqrt(jnp.float32(tlen)) * jnp.sqrt(power + EPS))
    me = lax.axis_index("tmpl")
    turns = LANES // STEP
    sources = [me] + [lookup([route.index(i) for i in range(owners)], me) for route in routes("tmpl", owners)]
    for p in range(pairs):
        m, j = p // slots, p % slots
        source, slot = entries[j, m] // capacity, entries[j, m] % capacity
        for i in range(owners):
            slot = jnp.where(source == sources[i], slot % capacity + i * ROWS, slot)
        shift = shifts[j, m]
        row_of = slot + (shift // LANES) * owners * ROWS
        table[p : p + 1, :] = jnp.full((1, LANES), row_of * LANES + (LANES - shift % LANES) % LANES)
        weight = factors[j, m].astype(jnp.float32)
        scale[p * groups : (p + 1) * groups, :] = jnp.broadcast_to(factor[p : p + 1] * weight, (groups, LANES))
    turned = [
        jnp.dot(values[:, d * LANES : (d + 1) * LANES].astype(jnp.bfloat16), mirror, preferred_element_type=jnp.float32)
        for d in range(-(-tlen // LANES))
    ]
    for c in range(pairs // turns):
        j, m = c // (count // turns), c % (count // turns) * turns
        before = zero
        for d in range(depth // LANES):
            now = zero
            if d * LANES < tlen:
                for h in range(turns):
                    back = turned[d][(m + h) * slots + j : (m + h) * slots + j + 1, :]
                    other = pltpu.roll(jnp.broadcast_to(back, (LANES, LANES)), 1 + h * STEP, axis=1, stride=1, stride_axis=0)
                    now = jnp.where(lane < h * STEP, now, other)
            bands[d * LANES : (d + 1) * LANES, c * LANES : (c + 1) * LANES] = jnp.where(late, now, before).astype(jnp.bfloat16)
            before = now
    for m in range(count):
        total = jnp.int32(0)
        for j in range(slots):
            total += factors[j, m] * factors[j, m]
        totals[m : m + 1, :] = jnp.full((1, LANES), total.astype(jnp.float32))


def correlate(owners, columns, tlen, count, slots, table, *refs):
    packed, refs = refs[:owners], refs[owners:]
    bands, box, scale, totals = refs[:4]
    outs, (lanes, stacks, sums, blocks) = refs[4:-4], refs[-4:]
    column = lax.axis_index("chan")
    pairs = count * slots
    depth = box.shape[0]
    pieces = packed[0].shape[1] // LANES
    stride = owners * ROWS
    groups = LAGS // STEP
    turns = LANES // STEP
    reach = LAGS // LANES + depth // LANES - 1
    for i in range(owners):
        wide = packed[i][...].astype(jnp.float32)
        for d in range(pieces):
            lanes[d * stride + i * ROWS : d * stride + (i + 1) * ROWS, :] = wide[:, d * LANES : (d + 1) * LANES]
    lanes[pieces * stride : (pieces + 1) * stride, :] = jnp.zeros((stride, LANES), jnp.float32)
    places = table[...]
    lane = lax.broadcasted_iota(jnp.int32, (reach, LANES), 1)
    for p in range(pairs):
        place = places[p, 0]
        first, back = lax.shift_right_logical(place, 7), lax.bitwise_and(place, LANES - 1)
        for h in range(turns):
            if h:
                first = jnp.where((back > 0) & (back <= STEP), first + stride, first)
                back = lax.bitwise_xor(back, STEP)
            low = lanes[pl.ds(first, reach, stride=stride), :]
            up = lanes[pl.ds(first + stride, reach, stride=stride), :]
            rest = lax.bitwise_and(LANES - back, LANES - 1)
            stacks[p, pl.ds(h, reach, stride=turns), :] = pltpu.roll(jnp.where(lane >= rest, low, up), back, axis=1)
    taps = [
        jnp.concatenate([stacks[p, d * turns : d * turns + groups, :] for d in range(depth // LANES)], axis=1) for p in range(pairs)
    ]
    taps = jnp.concatenate(taps, axis=0)
    product = jnp.dot(taps.astype(jnp.bfloat16), bands[...], preferred_element_type=jnp.float32)
    square = taps * taps
    main = square.astype(jnp.bfloat16)
    left = (square - main.astype(jnp.float32)).astype(jnp.bfloat16)
    energy = jnp.dot(jnp.concatenate([main, left], axis=0), box[...], preferred_element_type=jnp.float32)
    energy = energy[: pairs * groups] + energy[pairs * groups :]
    norm = scale[...] * lax.rsqrt(energy * (1.0 / tlen) + EPS)
    front = lax.broadcasted_iota(jnp.int32, (LAGS // LANES, LANES), 1) < STEP
    for m in range(count):
        both = jnp.zeros((groups, LANES), jnp.float32)
        for j in range(slots):
            rows = slice((m * slots + j) * groups, (m * slots + j + 1) * groups)
            c = j * (count // turns) + m // turns
            both += product[rows, c * LANES : (c + 1) * LANES] * norm[rows, :]
        sums[m, :groups, :] = both
        even = sums[m, pl.ds(0, LAGS // LANES, stride=turns), :]
        odd = sums[m, pl.ds(1, LAGS // LANES, stride=turns), :]
        if m % turns:
            even = pltpu.roll(even, STEP, axis=1)
        else:
            odd = pltpu.roll(odd, STEP, axis=1)
        blocks[: LAGS // LANES, m, :] = jnp.where(front, even, odd)
        blocks[: LAGS // LANES, count + m, :] = jnp.broadcast_to(totals[m : m + 1, :], (LAGS // LANES, LANES))
    width = LAGS // columns
    share = LANES // width

    def block(target):
        part = blocks[target // share]
        chosen = part[:, :width]
        for s in range(1, share):
            chosen = jnp.where(target % share == s, part[:, s * width : (s + 1) * width], chosen)
        return chosen

    outs[-1][...] = block(column)
    if ("chan", columns) in ROUTES:
        for out, route in zip(outs, routes("chan", columns)):
            out[...] = block(lookup(route, column))
        return
    distance = 1
    for out in outs[:-1]:
        for q in range(out.shape[0]):
            out[q] = block(column ^ (distance * (2 * q + 1)))
        distance *= 2


def shards(waveforms, templates, selection, channel_list, moveouts, weights):
    owners = lax.axis_size("tmpl")
    columns = lax.axis_size("chan")
    count, slots, tlen = templates.shape
    pairs = count * slots
    groups = LAGS // STEP
    width = LAGS // columns
    samples = waveforms.shape[1]
    capacity = selection.shape[3]
    depth = -(-(tlen + STEP - 1) // LANES) * LANES
    pieces = samples // LANES

    def call(kernel, name, ins, outs, scratch, arguments, cost=None):
        if ins is HBM:
            arguments = [pltpu.with_memory_space_constraint(x, pltpu.HBM) for x in arguments]
        single = not isinstance(outs, tuple)
        return pl.pallas_call(
            kernel,
            out_shape=outs,
            in_specs=[ins] * len(arguments),
            out_specs=VMEM if single else (VMEM,) * len(outs),
            scratch_shapes=scratch,
            compiler_params=PARAMS,
            cost_estimate=cost,
            name=name,
        )(*arguments)

    rows = jax.ShapeDtypeStruct((ROWS, samples), waveforms.dtype)
    own, *outgoing = call(
        pack,
        "pack",
        HBM,
        (rows,) * owners,
        [
            pltpu.VMEM(waveforms.shape, waveforms.dtype),
            pltpu.SMEM(selection.shape, selection.dtype),
            pltpu.SemaphoreType.DMA((2,)),
        ],
        (waveforms, selection),
    )
    bands, box, scale, totals, table = call(
        functools.partial(prepare, owners, capacity, tlen),
        "prepare",
        HBM,
        (
            jax.ShapeDtypeStruct((depth, pairs * STEP), jnp.bfloat16),
            jax.ShapeDtypeStruct((depth, LANES), jnp.bfloat16),
            jax.ShapeDtypeStruct((pairs * groups, LANES), jnp.float32),
            jax.ShapeDtypeStruct((count, LANES), jnp.float32),
            jax.ShapeDtypeStruct((pairs, LANES), jnp.int32),
        ),
        [
            pltpu.VMEM((pairs, depth), jnp.float32),
            pltpu.VMEM(templates.shape, templates.dtype),
            pltpu.SMEM((slots, count), jnp.int32),
            pltpu.SMEM((slots, count), jnp.int32),
            pltpu.SMEM((slots, count), jnp.int32),
            pltpu.SemaphoreType.DMA((4,)),
        ],
        (templates, channel_list.T, moveouts.T, weights.T),
        pl.CostEstimate(flops=2_000_000, bytes_accessed=2_000_000, transcendentals=0),
    )
    packed = [own] + [send(x, "tmpl", route) for x, route in zip(outgoing, routes("tmpl", owners))]
    sizes = []
    while (columns >> len(sizes)) > 1:
        sizes.append(columns >> (len(sizes) + 1))
    shapes = [(s, 2 * count, width) for s in sizes] + [(2 * count, width)]
    if ("chan", columns) in ROUTES:
        shapes = [(2 * count, width)] * columns
    parts = call(
        functools.partial(correlate, owners, columns, tlen, count, slots),
        "correlate",
        VMEM,
        tuple(jax.ShapeDtypeStruct(s, jnp.float32) for s in shapes),
        [
            pltpu.VMEM(((pieces + 8) * owners * ROWS, LANES), jnp.float32),
            pltpu.VMEM((pairs, 32, LANES), jnp.float32),
            pltpu.VMEM((count, 2 * groups, LANES), jnp.float32),
            pltpu.VMEM((2 * LAGS // LANES, 2 * count, LANES), jnp.float32),
        ],
        (table, *packed, bands, box, scale, totals),
    )
    stages, own = list(parts[:-1]), [parts[-1]]
    if ("chan", columns) in ROUTES:
        for part, route in zip(stages, routes("chan", columns)):
            own.append(send(part, "chan", route))
        stages = []
    for i in range(len(stages)):
        arrived = exchange(stages[i], "chan", 1 << i)
        own.append(arrived[0])
        for later in range(i + 1, len(stages)):
            step = 1 << (later - i)
            stages[later] = stages[later] + arrived[step // 2 :: step]
    top = sum(x[:count] for x in own)
    return top / jnp.sqrt(sum(x[count:] for x in own))


def solution(mesh):
    placed = (
        P(("parts", "tmpl", "chan"), None),
        P(("parts", "tmpl"), "chan", None),
        P(("parts", "tmpl"), "chan", None, None),
        P(("parts", "tmpl"), "chan"),
        P(("parts", "tmpl"), "chan"),
        P(("parts", "tmpl"), "chan"),
    )
    return jax.shard_map(
        shards, mesh=mesh, in_specs=placed, out_specs=P(("parts", "tmpl"), "chan"), check_vma=False
    )
```

```python
import functools

import jax
import jax.numpy as jnp
from jax import lax
from jax.experimental import pallas as pl
from jax.experimental.pallas import tpu as pltpu
from jax.sharding import PartitionSpec as P

LAGS = 512
EPS = 1e-06
LANES = 128
PARAMS = pltpu.CompilerParams(vmem_limit_bytes=8 * 1024 * 1024)
STEP = 64
ROUTES = {
    ("tmpl", 4): ((3, 2, 0, 1), (2, 3, 1, 0), (1, 0, 3, 2)),
    ("chan", 4): ((2, 3, 1, 0), (3, 2, 0, 1), (1, 0, 3, 2)),
}
ROWS = 8
VMEM = pl.BlockSpec(memory_space=pltpu.VMEM)
HBM = pl.BlockSpec(memory_space=pltpu.HBM)


def exchange(value, axis, distance):
    size = lax.axis_size(axis)
    return lax.ppermute(value, axis, [(i, i ^ distance) for i in range(size)])


def routes(axis, size):
    return ROUTES.get((axis, size), tuple(tuple(i ^ k for i in range(size)) for k in range(1, size)))


def send(value, axis, route):
    return lax.ppermute(value, axis, list(enumerate(route)))


def lookup(values, place):
    found = jnp.int32(values[0])
    for i in range(1, len(values)):
        found = jnp.where(place == i, values[i], found)
    return found


def fetch(sources, targets, sems):
    copies = [pltpu.make_async_copy(a, b, sems.at[i]) for i, (a, b) in enumerate(zip(sources, targets))]
    for copy in copies:
        copy.start()
    return copies


def pack(waveforms, selection, *refs):
    outs, (taken, choice, sems) = refs[:-3], refs[-3:]
    copies = fetch((waveforms, selection), (taken, choice), sems)
    high, samples = waveforms.shape
    _, _, owners, capacity = choice.shape
    me = lax.axis_index("tmpl")
    tall = -(-high // 16) * 16
    row = lax.broadcasted_iota(jnp.int32, (ROWS, tall), 0)
    column = lax.broadcasted_iota(jnp.int32, (ROWS, tall), 1)
    copies[1].wait()
    picks = []
    for route in (tuple(range(owners)),) + routes("tmpl", owners):
        target = lookup(route, me)
        local = jnp.full((ROWS, tall), -1, jnp.int32)
        for j in range(capacity):
            local = jnp.where(row == j, choice[0, 0, target, j], local)
        picks.append(jnp.where(local == column, 1.0, 0.0))
    picks = jnp.concatenate(picks, axis=0).astype(jnp.bfloat16)
    copies[0].wait()
    records = jnp.pad(taken[...].astype(jnp.float32), ((0, tall - high), (0, 0))).astype(jnp.bfloat16)
    picked = jnp.dot(picks, records, preferred_element_type=jnp.float32)
    for i, out in enumerate(outs):
        out[...] = picked[i * ROWS : (i + 1) * ROWS].astype(jnp.bfloat16)


def prepare(
    owners, capacity, tlen, templates, lists, moveouts, weights, bands, box, scale, totals, table, rows, taken, entries, shifts, factors, sems
):
    copies = fetch((templates, lists, moveouts, weights), (taken, entries, shifts, factors), sems)
    count, slots, _ = taken.shape
    pairs = count * slots
    depth = box.shape[0]
    groups = LAGS // STEP
    tap = lax.broadcasted_iota(jnp.int32, (depth, LANES), 0) - lax.broadcasted_iota(jnp.int32, (depth, LANES), 1) % STEP
    box[...] = jnp.where((tap >= 0) & (tap < tlen), 1.0, 0.0).astype(jnp.bfloat16)
    rows[...] = jnp.zeros_like(rows)
    for copy in copies:
        copy.wait()
    for m in range(count):
        rows[m * slots : (m + 1) * slots, :tlen] = taken[m].astype(jnp.float32)
    row = lax.broadcasted_iota(jnp.int32, (LANES, LANES), 0)
    lane = lax.broadcasted_iota(jnp.int32, (LANES, LANES), 1)
    late = row >= lane % STEP
    mirror = jnp.where(row + lane == LANES - 1, 1.0, 0.0).astype(jnp.bfloat16)
    zero = jnp.zeros((LANES, LANES), jnp.float32)
    values = rows[...]
    power = jnp.sum(values * values, axis=1, keepdims=True) / tlen
    factor = 1.0 / (jnp.sqrt(jnp.float32(tlen)) * jnp.sqrt(power + EPS))
    me = lax.axis_index("tmpl")
    turns = LANES // STEP
    sources = [me] + [lookup([route.index(i) for i in range(owners)], me) for route in routes("tmpl", owners)]
    for p in range(pairs):
        m, j = p // slots, p % slots
        source, slot = entries[j, m] // capacity, entries[j, m] % capacity
        for i in range(owners):
            slot = jnp.where(source == sources[i], slot % capacity + i * ROWS, slot)
        shift = shifts[j, m]
        row_of = slot + (shift // LANES) * owners * ROWS
        table[p : p + 1, :] = jnp.full((1, LANES), row_of * LANES + (LANES - shift % LANES) % LANES)
        weight = factors[j, m].astype(jnp.float32)
        scale[p * groups : (p + 1) * groups, :] = jnp.broadcast_to(factor[p : p + 1] * weight, (groups, LANES))
    turned = [
        jnp.dot(values[:, d * LANES : (d + 1) * LANES].astype(jnp.bfloat16), mirror, preferred_element_type=jnp.float32)
        for d in range(-(-tlen // LANES))
    ]
    for c in range(pairs // turns):
        j, m = c // (count // turns), c % (count // turns) * turns
        before = zero
        for d in range(depth // LANES):
            now = zero
            if d * LANES < tlen:
                for h in range(turns):
                    back = turned[d][(m + h) * slots + j : (m + h) * slots + j + 1, :]
                    other = pltpu.roll(jnp.broadcast_to(back, (LANES, LANES)), 1 + h * STEP, axis=1, stride=1, stride_axis=0)
                    now = jnp.where(lane < h * STEP, now, other)
            bands[d * LANES : (d + 1) * LANES, c * LANES : (c + 1) * LANES] = jnp.where(late, now, before).astype(jnp.bfloat16)
            before = now
    for m in range(count):
        total = jnp.int32(0)
        for j in range(slots):
            total += factors[j, m] * factors[j, m]
        totals[m : m + 1, :] = jnp.full((1, LANES), total.astype(jnp.float32))


def correlate(owners, columns, tlen, count, slots, table, *refs):
    packed, refs = refs[:owners], refs[owners:]
    bands, box, scale, totals = refs[:4]
    outs, (lanes, stacks, sums, blocks) = refs[4:-4], refs[-4:]
    column = lax.axis_index("chan")
    pairs = count * slots
    depth = box.shape[0]
    pieces = packed[0].shape[1] // LANES
    stride = owners * ROWS
    groups = LAGS // STEP
    turns = LANES // STEP
    reach = LAGS // LANES + depth // LANES - 1
    for i in range(owners):
        wide = packed[i][...].astype(jnp.float32)
        for d in range(pieces):
            lanes[d * stride + i * ROWS : d * stride + (i + 1) * ROWS, :] = wide[:, d * LANES : (d + 1) * LANES]
    lanes[pieces * stride : (pieces + 1) * stride, :] = jnp.zeros((stride, LANES), jnp.float32)
    places = table[...]
    lane = lax.broadcasted_iota(jnp.int32, (reach, LANES), 1)
    for p in range(pairs):
        place = places[p, 0]
        first, back = lax.shift_right_logical(place, 7), lax.bitwise_and(place, LANES - 1)
        for h in range(turns):
            if h:
                first = jnp.where((back > 0) & (back <= STEP), first + stride, first)
                back = lax.bitwise_xor(back, STEP)
            low = lanes[pl.ds(first, reach, stride=stride), :]
            up = lanes[pl.ds(first + stride, reach, stride=stride), :]
            rest = lax.bitwise_and(LANES - back, LANES - 1)
            stacks[p, pl.ds(h, reach, stride=turns), :] = pltpu.roll(jnp.where(lane >= rest, low, up), back, axis=1)
    taps = [
        jnp.concatenate([stacks[p, d * turns : d * turns + groups, :] for d in range(depth // LANES)], axis=1) for p in range(pairs)
    ]
    used = -(-(tlen + STEP - 1) // 16) * 16
    taps = jnp.concatenate(taps, axis=0)[:, :used]
    product = jnp.dot(taps.astype(jnp.bfloat16), bands[:used, :], preferred_element_type=jnp.float32)
    square = taps * taps
    main = square.astype(jnp.bfloat16)
    left = (square - main.astype(jnp.float32)).astype(jnp.bfloat16)
    energy = jnp.dot(jnp.concatenate([main, left], axis=0), box[:used, :], preferred_element_type=jnp.float32)
    energy = energy[: pairs * groups] + energy[pairs * groups :]
    norm = scale[...] * lax.rsqrt(energy * (1.0 / tlen) + EPS)
    front = lax.broadcasted_iota(jnp.int32, (LAGS // LANES, LANES), 1) < STEP
    for m in range(count):
        both = jnp.zeros((groups, LANES), jnp.float32)
        for j in range(slots):
            rows = slice((m * slots + j) * groups, (m * slots + j + 1) * groups)
            c = j * (count // turns) + m // turns
            both += product[rows, c * LANES : (c + 1) * LANES] * norm[rows, :]
        sums[m, :groups, :] = both
        even = sums[m, pl.ds(0, LAGS // LANES, stride=turns), :]
        odd = sums[m, pl.ds(1, LAGS // LANES, stride=turns), :]
        if m % turns:
            even = pltpu.roll(even, STEP, axis=1)
        else:
            odd = pltpu.roll(odd, STEP, axis=1)
        blocks[: LAGS // LANES, m, :] = jnp.where(front, even, odd)
        blocks[: LAGS // LANES, count + m, :] = jnp.broadcast_to(totals[m : m + 1, :], (LAGS // LANES, LANES))
    width = LAGS // columns
    share = LANES // width

    def block(target):
        part = blocks[target // share]
        chosen = part[:, :width]
        for s in range(1, share):
            chosen = jnp.where(target % share == s, part[:, s * width : (s + 1) * width], chosen)
        return chosen

    outs[-1][...] = block(column)
    if ("chan", columns) in ROUTES:
        for out, route in zip(outs, routes("chan", columns)):
            out[...] = block(lookup(route, column))
        return
    distance = 1
    for out in outs[:-1]:
        for q in range(out.shape[0]):
            out[q] = block(column ^ (distance * (2 * q + 1)))
        distance *= 2


def shards(waveforms, templates, selection, channel_list, moveouts, weights):
    owners = lax.axis_size("tmpl")
    columns = lax.axis_size("chan")
    count, slots, tlen = templates.shape
    pairs = count * slots
    groups = LAGS // STEP
    width = LAGS // columns
    samples = waveforms.shape[1]
    capacity = selection.shape[3]
    depth = -(-(tlen + STEP - 1) // LANES) * LANES
    pieces = samples // LANES

    def call(kernel, name, ins, outs, scratch, arguments, cost=None):
        if ins is HBM:
            arguments = [pltpu.with_memory_space_constraint(x, pltpu.HBM) for x in arguments]
        single = not isinstance(outs, tuple)
        return pl.pallas_call(
            kernel,
            out_shape=outs,
            in_specs=[ins] * len(arguments),
            out_specs=VMEM if single else (VMEM,) * len(outs),
            scratch_shapes=scratch,
            compiler_params=PARAMS,
            cost_estimate=cost,
            name=name,
        )(*arguments)

    rows = jax.ShapeDtypeStruct((ROWS, samples), waveforms.dtype)
    own, *outgoing = call(
        pack,
        "pack",
        HBM,
        (rows,) * owners,
        [
            pltpu.VMEM(waveforms.shape, waveforms.dtype),
            pltpu.SMEM(selection.shape, selection.dtype),
            pltpu.SemaphoreType.DMA((2,)),
        ],
        (waveforms, selection),
    )
    bands, box, scale, totals, table = call(
        functools.partial(prepare, owners, capacity, tlen),
        "prepare",
        HBM,
        (
            jax.ShapeDtypeStruct((depth, pairs * STEP), jnp.bfloat16),
            jax.ShapeDtypeStruct((depth, LANES), jnp.bfloat16),
            jax.ShapeDtypeStruct((pairs * groups, LANES), jnp.float32),
            jax.ShapeDtypeStruct((count, LANES), jnp.float32),
            jax.ShapeDtypeStruct((pairs, LANES), jnp.int32),
        ),
        [
            pltpu.VMEM((pairs, depth), jnp.float32),
            pltpu.VMEM(templates.shape, templates.dtype),
            pltpu.SMEM((slots, count), jnp.int32),
            pltpu.SMEM((slots, count), jnp.int32),
            pltpu.SMEM((slots, count), jnp.int32),
            pltpu.SemaphoreType.DMA((4,)),
        ],
        (templates, channel_list.T, moveouts.T, weights.T),
        pl.CostEstimate(flops=2_000_000, bytes_accessed=2_000_000, transcendentals=0),
    )
    packed = [own] + [send(x, "tmpl", route) for x, route in zip(outgoing, routes("tmpl", owners))]
    sizes = []
    while (columns >> len(sizes)) > 1:
        sizes.append(columns >> (len(sizes) + 1))
    shapes = [(s, 2 * count, width) for s in sizes] + [(2 * count, width)]
    if ("chan", columns) in ROUTES:
        shapes = [(2 * count, width)] * columns
    parts = call(
        functools.partial(correlate, owners, columns, tlen, count, slots),
        "correlate",
        VMEM,
        tuple(jax.ShapeDtypeStruct(s, jnp.float32) for s in shapes),
        [
            pltpu.VMEM(((pieces + 8) * owners * ROWS, LANES), jnp.float32),
            pltpu.VMEM((pairs, 32, LANES), jnp.float32),
            pltpu.VMEM((count, 2 * groups, LANES), jnp.float32),
            pltpu.VMEM((2 * LAGS // LANES, 2 * count, LANES), jnp.float32),
        ],
        (table, *packed, bands, box, scale, totals),
    )
    stages, own = list(parts[:-1]), [parts[-1]]
    if ("chan", columns) in ROUTES:
        for part, route in zip(stages, routes("chan", columns)):
            own.append(send(part, "chan", route))
        stages = []
    for i in range(len(stages)):
        arrived = exchange(stages[i], "chan", 1 << i)
        own.append(arrived[0])
        for later in range(i + 1, len(stages)):
            step = 1 << (later - i)
            stages[later] = stages[later] + arrived[step // 2 :: step]
    top = sum(x[:count] for x in own)
    return top / jnp.sqrt(sum(x[count:] for x in own))


def solution(mesh):
    placed = (
        P(("parts", "tmpl", "chan"), None),
        P(("parts", "tmpl"), "chan", None),
        P(("parts", "tmpl"), "chan", None, None),
        P(("parts", "tmpl"), "chan"),
        P(("parts", "tmpl"), "chan"),
        P(("parts", "tmpl"), "chan"),
    )
    return jax.shard_map(
        shards, mesh=mesh, in_specs=placed, out_specs=P(("parts", "tmpl"), "chan"), check_vma=False
    )
```

```python
import functools

import jax
import jax.numpy as jnp
from jax import lax
from jax.experimental import pallas as pl
from jax.experimental.pallas import tpu as pltpu
from jax.sharding import PartitionSpec as P

LAGS = 512
EPS = 1e-06
LANES = 128
PARAMS = pltpu.CompilerParams(vmem_limit_bytes=8 * 1024 * 1024)
STEP = 64
ROUTES = {
    ("tmpl", 4): ((3, 2, 0, 1), (2, 3, 1, 0), (1, 0, 3, 2)),
    ("chan", 4): ((2, 3, 1, 0), (3, 2, 0, 1), (1, 0, 3, 2)),
}
ROWS = 8
VMEM = pl.BlockSpec(memory_space=pltpu.VMEM)
HBM = pl.BlockSpec(memory_space=pltpu.HBM)


def exchange(value, axis, distance):
    size = lax.axis_size(axis)
    return lax.ppermute(value, axis, [(i, i ^ distance) for i in range(size)])


def routes(axis, size):
    return ROUTES.get((axis, size), tuple(tuple(i ^ k for i in range(size)) for k in range(1, size)))


def send(value, axis, route):
    return lax.ppermute(value, axis, list(enumerate(route)))


def lookup(values, place):
    found = jnp.int32(values[0])
    for i in range(1, len(values)):
        found = jnp.where(place == i, values[i], found)
    return found


def fetch(sources, targets, sems):
    copies = [pltpu.make_async_copy(a, b, sems.at[i]) for i, (a, b) in enumerate(zip(sources, targets))]
    for copy in copies:
        copy.start()
    return copies


def pack(waveforms, selection, *refs):
    outs, (taken, choice, sems) = refs[:-3], refs[-3:]
    copies = fetch((waveforms, selection), (taken, choice), sems)
    high, samples = waveforms.shape
    _, _, owners, capacity = choice.shape
    me = lax.axis_index("tmpl")
    tall = -(-high // 16) * 16
    row = lax.broadcasted_iota(jnp.int32, (ROWS, tall), 0)
    column = lax.broadcasted_iota(jnp.int32, (ROWS, tall), 1)
    for copy in copies:
        copy.wait()
    picks = []
    for route in (tuple(range(owners)),) + routes("tmpl", owners):
        target = lookup(route, me)
        local = jnp.full((ROWS, tall), -1, jnp.int32)
        for j in range(capacity):
            local = jnp.where(row == j, choice[0, 0, target, j], local)
        picks.append(jnp.where(local == column, 1.0, 0.0))
    picks = jnp.concatenate(picks, axis=0).astype(jnp.bfloat16)
    records = jnp.pad(taken[...].astype(jnp.float32), ((0, tall - high), (0, 0))).astype(jnp.bfloat16)
    picked = jnp.dot(picks, records, preferred_element_type=jnp.float32)
    for i, out in enumerate(outs):
        out[...] = picked[i * ROWS : (i + 1) * ROWS].astype(jnp.bfloat16)


def prepare(
    owners, capacity, tlen, templates, lists, moveouts, weights, bands, box, scale, totals, table, rows, taken, entries, shifts, factors, sems
):
    copies = fetch((templates, lists, moveouts, weights), (taken, entries, shifts, factors), sems)
    count, slots, _ = taken.shape
    pairs = count * slots
    depth = box.shape[0]
    groups = LAGS // STEP
    tap = lax.broadcasted_iota(jnp.int32, (depth, LANES), 0) - lax.broadcasted_iota(jnp.int32, (depth, LANES), 1) % STEP
    box[...] = jnp.where((tap >= 0) & (tap < tlen), 1.0, 0.0).astype(jnp.bfloat16)
    rows[...] = jnp.zeros_like(rows)
    for copy in copies:
        copy.wait()
    for m in range(count):
        rows[m * slots : (m + 1) * slots, :tlen] = taken[m].astype(jnp.float32)
    row = lax.broadcasted_iota(jnp.int32, (LANES, LANES), 0)
    lane = lax.broadcasted_iota(jnp.int32, (LANES, LANES), 1)
    late = row >= lane % STEP
    mirror = jnp.where(row + lane == LANES - 1, 1.0, 0.0).astype(jnp.bfloat16)
    zero = jnp.zeros((LANES, LANES), jnp.float32)
    values = rows[...]
    power = jnp.sum(values * values, axis=1, keepdims=True) / tlen
    factor = 1.0 / (jnp.sqrt(jnp.float32(tlen)) * jnp.sqrt(power + EPS))
    me = lax.axis_index("tmpl")
    turns = LANES // STEP
    sources = [me] + [lookup([route.index(i) for i in range(owners)], me) for route in routes("tmpl", owners)]
    for p in range(pairs):
        m, j = p // slots, p % slots
        source, slot = entries[j, m] // capacity, entries[j, m] % capacity
        for i in range(owners):
            slot = jnp.where(source == sources[i], slot % capacity + i * ROWS, slot)
        shift = shifts[j, m]
        row_of = slot + (shift // LANES) * owners * ROWS
        table[p : p + 1, :] = jnp.full((1, LANES), row_of * LANES + (LANES - shift % LANES) % LANES)
        weight = factors[j, m].astype(jnp.float32)
        scale[p * groups : (p + 1) * groups, :] = jnp.broadcast_to(factor[p : p + 1] * weight, (groups, LANES))
    turned = [
        jnp.dot(values[:, d * LANES : (d + 1) * LANES].astype(jnp.bfloat16), mirror, preferred_element_type=jnp.float32)
        for d in range(-(-tlen // LANES))
    ]
    for c in range(pairs // turns):
        j, m = c // (count // turns), c % (count // turns) * turns
        before = zero
        for d in range(depth // LANES):
            now = zero
            if d * LANES < tlen:
                for h in range(turns):
                    back = turned[d][(m + h) * slots + j : (m + h) * slots + j + 1, :]
                    other = pltpu.roll(jnp.broadcast_to(back, (LANES, LANES)), 1 + h * STEP, axis=1, stride=1, stride_axis=0)
                    now = jnp.where(lane < h * STEP, now, other)
            bands[d * LANES : (d + 1) * LANES, c * LANES : (c + 1) * LANES] = jnp.where(late, now, before).astype(jnp.bfloat16)
            before = now
    for m in range(count):
        total = jnp.int32(0)
        for j in range(slots):
            total += factors[j, m] * factors[j, m]
        totals[m : m + 1, :] = jnp.full((1, LANES), total.astype(jnp.float32))


def correlate(owners, columns, tlen, count, slots, table, *refs):
    packed, refs = refs[:owners], refs[owners:]
    bands, box, scale, totals = refs[:4]
    outs, (lanes, stacks, sums, blocks) = refs[4:-4], refs[-4:]
    column = lax.axis_index("chan")
    pairs = count * slots
    depth = box.shape[0]
    pieces = packed[0].shape[1] // LANES
    stride = owners * ROWS
    groups = LAGS // STEP
    turns = LANES // STEP
    reach = LAGS // LANES + depth // LANES - 1
    for i in range(owners):
        wide = packed[i][...].astype(jnp.float32)
        for d in range(pieces):
            lanes[d * stride + i * ROWS : d * stride + (i + 1) * ROWS, :] = wide[:, d * LANES : (d + 1) * LANES]
    lanes[pieces * stride : (pieces + 1) * stride, :] = jnp.zeros((stride, LANES), jnp.float32)
    places = table[...]
    lane = lax.broadcasted_iota(jnp.int32, (reach, LANES), 1)
    for p in range(pairs):
        place = places[p, 0]
        first, back = lax.shift_right_logical(place, 7), lax.bitwise_and(place, LANES - 1)
        for h in range(turns):
            if h:
                first = jnp.where((back > 0) & (back <= STEP), first + stride, first)
                back = lax.bitwise_xor(back, STEP)
            low = lanes[pl.ds(first, reach, stride=stride), :]
            up = lanes[pl.ds(first + stride, reach, stride=stride), :]
            rest = lax.bitwise_and(LANES - back, LANES - 1)
            stacks[p, pl.ds(h, reach, stride=turns), :] = pltpu.roll(jnp.where(lane >= rest, low, up), back, axis=1)
    taps = [
        jnp.concatenate([stacks[p, d * turns : d * turns + groups, :] for d in range(depth // LANES)], axis=1) for p in range(pairs)
    ]
    used = -(-(tlen + STEP - 1) // 16) * 16
    taps = jnp.concatenate(taps, axis=0)[:, :used]
    short = taps.astype(jnp.bfloat16)
    half = pairs * STEP // 2
    product = [jnp.dot(short, bands[:used, i * half : (i + 1) * half], preferred_element_type=jnp.float32) for i in range(2)]
    product = jnp.concatenate(product, axis=1)
    square = taps * taps
    main = square.astype(jnp.bfloat16)
    left = (square - main.astype(jnp.float32)).astype(jnp.bfloat16)
    energy = jnp.dot(jnp.concatenate([main, left], axis=0), box[:used, :], preferred_element_type=jnp.float32)
    energy = energy[: pairs * groups] + energy[pairs * groups :]
    norm = scale[...] * lax.rsqrt(energy * (1.0 / tlen) + EPS)
    front = lax.broadcasted_iota(jnp.int32, (LAGS // LANES, LANES), 1) < STEP
    for m in range(count):
        both = jnp.zeros((groups, LANES), jnp.float32)
        for j in range(slots):
            rows = slice((m * slots + j) * groups, (m * slots + j + 1) * groups)
            c = j * (count // turns) + m // turns
            both += product[rows, c * LANES : (c + 1) * LANES] * norm[rows, :]
        sums[m, :groups, :] = both
        even = sums[m, pl.ds(0, LAGS // LANES, stride=turns), :]
        odd = sums[m, pl.ds(1, LAGS // LANES, stride=turns), :]
        if m % turns:
            even = pltpu.roll(even, STEP, axis=1)
        else:
            odd = pltpu.roll(odd, STEP, axis=1)
        blocks[: LAGS // LANES, m, :] = jnp.where(front, even, odd)
        blocks[: LAGS // LANES, count + m, :] = jnp.broadcast_to(totals[m : m + 1, :], (LAGS // LANES, LANES))
    width = LAGS // columns
    share = LANES // width

    def block(target):
        part = blocks[target // share]
        chosen = part[:, :width]
        for s in range(1, share):
            chosen = jnp.where(target % share == s, part[:, s * width : (s + 1) * width], chosen)
        return chosen

    outs[-1][...] = block(column)
    if ("chan", columns) in ROUTES:
        for out, route in zip(outs, routes("chan", columns)):
            out[...] = block(lookup(route, column))
        return
    distance = 1
    for out in outs[:-1]:
        for q in range(out.shape[0]):
            out[q] = block(column ^ (distance * (2 * q + 1)))
        distance *= 2


def shards(waveforms, templates, selection, channel_list, moveouts, weights):
    owners = lax.axis_size("tmpl")
    columns = lax.axis_size("chan")
    count, slots, tlen = templates.shape
    pairs = count * slots
    groups = LAGS // STEP
    width = LAGS // columns
    samples = waveforms.shape[1]
    capacity = selection.shape[3]
    depth = -(-(tlen + STEP - 1) // LANES) * LANES
    pieces = samples // LANES

    def call(kernel, name, ins, outs, scratch, arguments, cost=None):
        if ins is HBM:
            arguments = [pltpu.with_memory_space_constraint(x, pltpu.HBM) for x in arguments]
        single = not isinstance(outs, tuple)
        return pl.pallas_call(
            kernel,
            out_shape=outs,
            in_specs=[ins] * len(arguments),
            out_specs=VMEM if single else (VMEM,) * len(outs),
            scratch_shapes=scratch,
            compiler_params=PARAMS,
            cost_estimate=cost,
            name=name,
        )(*arguments)

    rows = jax.ShapeDtypeStruct((ROWS, samples), waveforms.dtype)
    own, *outgoing = call(
        pack,
        "pack",
        HBM,
        (rows,) * owners,
        [
            pltpu.VMEM(waveforms.shape, waveforms.dtype),
            pltpu.SMEM(selection.shape, selection.dtype),
            pltpu.SemaphoreType.DMA((2,)),
        ],
        (waveforms, selection),
    )
    bands, box, scale, totals, table = call(
        functools.partial(prepare, owners, capacity, tlen),
        "prepare",
        HBM,
        (
            jax.ShapeDtypeStruct((depth, pairs * STEP), jnp.bfloat16),
            jax.ShapeDtypeStruct((depth, LANES), jnp.bfloat16),
            jax.ShapeDtypeStruct((pairs * groups, LANES), jnp.float32),
            jax.ShapeDtypeStruct((count, LANES), jnp.float32),
            jax.ShapeDtypeStruct((pairs, LANES), jnp.int32),
        ),
        [
            pltpu.VMEM((pairs, depth), jnp.float32),
            pltpu.VMEM(templates.shape, templates.dtype),
            pltpu.SMEM((slots, count), jnp.int32),
            pltpu.SMEM((slots, count), jnp.int32),
            pltpu.SMEM((slots, count), jnp.int32),
            pltpu.SemaphoreType.DMA((4,)),
        ],
        (templates, channel_list.T, moveouts.T, weights.T),
        pl.CostEstimate(flops=2_000_000, bytes_accessed=2_000_000, transcendentals=0),
    )
    packed = [own] + [send(x, "tmpl", route) for x, route in zip(outgoing, routes("tmpl", owners))]
    sizes = []
    while (columns >> len(sizes)) > 1:
        sizes.append(columns >> (len(sizes) + 1))
    shapes = [(s, 2 * count, width) for s in sizes] + [(2 * count, width)]
    if ("chan", columns) in ROUTES:
        shapes = [(2 * count, width)] * columns
    parts = call(
        functools.partial(correlate, owners, columns, tlen, count, slots),
        "correlate",
        VMEM,
        tuple(jax.ShapeDtypeStruct(s, jnp.float32) for s in shapes),
        [
            pltpu.VMEM(((pieces + 8) * owners * ROWS, LANES), jnp.float32),
            pltpu.VMEM((pairs, 32, LANES), jnp.float32),
            pltpu.VMEM((count, 2 * groups, LANES), jnp.float32),
            pltpu.VMEM((2 * LAGS // LANES, 2 * count, LANES), jnp.float32),
        ],
        (table, *packed, bands, box, scale, totals),
    )
    stages, own = list(parts[:-1]), [parts[-1]]
    if ("chan", columns) in ROUTES:
        for part, route in zip(stages, routes("chan", columns)):
            own.append(send(part, "chan", route))
        stages = []
    for i in range(len(stages)):
        arrived = exchange(stages[i], "chan", 1 << i)
        own.append(arrived[0])
        for later in range(i + 1, len(stages)):
            step = 1 << (later - i)
            stages[later] = stages[later] + arrived[step // 2 :: step]
    top = sum(x[:count] for x in own)
    return top / jnp.sqrt(sum(x[count:] for x in own))


def solution(mesh):
    placed = (
        P(("parts", "tmpl", "chan"), None),
        P(("parts", "tmpl"), "chan", None),
        P(("parts", "tmpl"), "chan", None, None),
        P(("parts", "tmpl"), "chan"),
        P(("parts", "tmpl"), "chan"),
        P(("parts", "tmpl"), "chan"),
    )
    return jax.shard_map(
        shards, mesh=mesh, in_specs=placed, out_specs=P(("parts", "tmpl"), "chan"), check_vma=False
    )
```
